512 devices in a mesh: chan: 64 (over y_hi, z, x), hour: 8 (over y_lo, core).
Axes of the slice: x: 4, y: 8 (y_hi: 2, y_lo: 4; y = y_hi * 4 + y_lo), z: 8, core: 2. Of those that a mesh axis runs over, the one named last changes fastest.
Arguments:
- raw: float32 [8, 1536, 1024], P('hour', 'chan'), may hold values from -700 to 700
Outputs:
- stack: float32 [1024, 63, 1024], P('chan', None, 'hour')
The draws below stay inside these ranges and needn't reach their ends.
All inputs are finite; a program needn't handle non-finite values.
Results may differ from the reference program's by a relative error of at most 0.00011.
Values sent between devices are 32-bit elements; how exact they have to be, the bound alone decides.
No kernel may reach another device: no remote copies, remote signals or barrier semaphores. Data moves between devices by JAX's collectives and lax.ppermute only.
A program may use at most 64 MiB of HBM per device.

```python
import math
import jax
import jax.numpy as jnp
from jax import lax

C = 1024
MAXLAG = 31
HALF = 64
LAGS = 63
SAMPLES = 1536
HOURS = 8


def draw_raw(key, part):
    key = jax.random.fold_in(key, 11)
    key_noise, key_env, key_scale, key_offset = jax.random.split(key, 4)
    envelope = jnp.exp(jax.random.uniform(key_env, (HOURS, SAMPLES // 16, C), jnp.float32) * math.log(10.0))
    envelope = jnp.repeat(envelope, 16, axis=1)
    scale = jnp.exp(jax.random.uniform(key_scale, (C,), jnp.float32) * math.log(10.0))
    offset = jnp.clip(jax.random.normal(key_offset, (C,), jnp.float32), -2.0, 2.0) * 1.5
    noise = jnp.clip(jax.random.normal(key_noise, (HOURS, SAMPLES, C), jnp.float32), -6.0, 6.0)
    return ((offset + noise * envelope) * scale).astype(jnp.float32)


def setup_inputs(seed: int = 0) -> dict:
    splits = jax.random.split(jax.random.key(seed), 2)
    return {
        "raw": draw_raw(jax.random.fold_in(splits[1], 71), 0),
    }


epsilon = 1e-6


def normalize(block):
    length = block.shape[-1]
    demeaned = block - jnp.mean(block, axis=-1, keepdims=True)
    magnitude = jnp.abs(demeaned)
    index = jnp.arange(length, dtype=jnp.int32)
    band = (jnp.abs(index[:, None] - index[None, :]) <= HALF).astype(jnp.float32)
    count = jnp.sum(band, axis=0)
    flat = magnitude.reshape(-1, length)
    running = jnp.dot(flat, band, precision=lax.Precision.HIGHEST).reshape(magnitude.shape) / count
    return demeaned / (running + epsilon)


def expand(normed):
    length = normed.shape[-1]
    widths = [(0, 0)] * (normed.ndim - 1) + [(MAXLAG, MAXLAG)]
    padded = jnp.pad(normed, widths)
    return jnp.stack([padded[..., 2 * MAXLAG - j: 2 * MAXLAG - j + length] for j in range(LAGS)], axis=-2)


def reference(raw):
    def step(total, frame):
        normed = normalize(frame.T)
        expanded = expand(normed)
        corr = jnp.einsum('pjt,qt->pjq', expanded, normed, precision=lax.Precision.HIGHEST)
        return total + corr, None

    total, _ = lax.scan(step, jnp.zeros((C, LAGS, C), jnp.float32), raw)
    return total * (1.0 / SAMPLES)
```

```python
import jax
import jax.numpy as jnp
from jax import lax
from jax.experimental import pallas as pl
from jax.experimental.pallas import tpu as pltpu
from jax.sharding import Mesh, PartitionSpec as P

C = 1024
MAXLAG = 31
HALF = 64
LAGS = 63
SAMPLES = 1536
epsilon = 1e-06

TAU = 24
ROW = SAMPLES + 32
K = 6400
FRONT = 40
QFRONT = FRONT - 24
SEQ = K + 128
CHUNK = 1280
ROT = (4, 8, 36, 40)
VMEM = pl.BlockSpec(memory_space=pltpu.VMEM)
SMEM = pl.BlockSpec(memory_space=pltpu.SMEM)
BIG = 56 * 1024 * 1024


def lanes(shape):
    return lax.broadcasted_iota(jnp.int32, shape, len(shape) - 1)


def prepack(raw, out):
    lane = lanes((TAU, 128))
    for low in range(4):
        a = raw[:, 256 * low : 256 * low + 128]
        b = raw[:, 256 * low + 128 : 256 * low + 256]
        first = jnp.where(
            lane < 32, a, jnp.where(lane < 64, pltpu.roll(b, 32, 1), jnp.where(lane < 96, pltpu.roll(a, 32, 1), pltpu.roll(b, 64, 1)))
        )
        second = jnp.where(
            lane < 32, pltpu.roll(a, 64, 1), jnp.where(lane < 64, pltpu.roll(b, 96, 1), jnp.where(lane < 96, pltpu.roll(a, 96, 1), b))
        )
        for high in range(2):
            out[4 * high + low, :, 512:640] = first
            out[4 * high + low, :, 640:768] = second
            out[4 * high + low, :, 0:512] = raw[:, 512 * high : 512 * high + 512]


def repack(got, p_out, q_out):
    low = lanes((TAU, 128)) < 64
    for high in range(2):
        for pair in range(2):
            one, two = 4 * high + 2 * pair, 4 * high + 2 * pair + 1
            for v in range(6):
                a = got[one, :, 128 * v : 128 * v + 128]
                b = got[two, :, 128 * v : 128 * v + 128]
                even = jnp.where(low, a, pltpu.roll(b, 64, 1))
                odd = jnp.where(low, pltpu.roll(a, 64, 1), b)
                if v < 4:
                    p_out[2 * v, high, pair] = even
                    p_out[2 * v + 1, high, pair] = odd
                else:
                    q_out[2 * (v - 4), high, pair] = even
                    q_out[2 * (v - 4) + 1, high, pair] = odd


def split(x):
    hi = x.astype(jnp.bfloat16)
    return hi, (x - hi.astype(jnp.float32)).astype(jnp.bfloat16)


def normalize(rec, mag):
    row = lax.broadcasted_iota(jnp.int32, (128, 256), 0)
    col = lanes((128, 256))
    band = jnp.where((col >= row) & (col <= row + 2 * HALF), 1.0, 0.0).astype(jnp.bfloat16)
    zero = jnp.zeros((HALF, 256), jnp.bfloat16)
    mag[0:HALF, :] = zero
    mag[HALF + SAMPLES : 2 * HALF + SAMPLES, :] = zero
    for pair in range(2):
        mean = jnp.sum(rec[pair], axis=0, keepdims=True) * (1.0 / SAMPLES)
        for i in range(12):
            d = rec[pair, 128 * i : 128 * i + 128, :] - mean
            rec[pair, 128 * i : 128 * i + 128, :] = d
            hi, lo = split(jnp.abs(d))
            mag[HALF + 128 * i : HALF + 128 * i + 128, 0:128] = hi
            mag[HALF + 128 * i : HALF + 128 * i + 128, 128:256] = lo
        for i in range(12):
            both = jnp.dot(band, mag[128 * i : 128 * i + 256, :], preferred_element_type=jnp.float32)
            t = lax.broadcasted_iota(jnp.int32, (128, 128), 0) + 128 * i
            count = (jnp.minimum(t, HALF) + jnp.minimum(SAMPLES - 1 - t, HALF) + 1).astype(jnp.float32)
            running = (both[:, 0:128] + both[:, 128:256]) / count
            rec[pair, 128 * i : 128 * i + 128, :] = rec[pair, 128 * i : 128 * i + 128, :] / (running + epsilon)


def p_kernel(me, p0, p1, p2, p3, hi_out, lo_out, rec, mag, seq, turned):
    for d, ref in enumerate((p0, p1, p2, p3)):
        x = lax.rem(me[0] + 4 - d, 4)
        for high in range(2):
            for z in range(8):
                at = pl.multiple_of(((high * 8 + z) * 4) * TAU + x * TAU, 8)
                for pair in range(2):
                    rec[pair, pl.ds(at, TAU), :] = ref[z, high, pair]
    normalize(rec, mag)
    seq[...] = jnp.zeros_like(seq)
    for pair in range(2):
        for i in range(12):
            x = rec[pair, 128 * i : 128 * i + 128, :]
            r = pltpu.roll(x, 64, 1)
            at = FRONT + 2 * pair * ROW + 128 * i
            seq[at : at + 128, 0:64] = x[:, 0:64]
            seq[at - 16 : at + 112, 64:128] = r[:, 64:128]
            at += ROW
            seq[at : at + 128, 0:64] = r[:, 0:64]
            seq[at - 16 : at + 112, 64:128] = x[:, 64:128]
    for i in range(SEQ // 128):
        turned[:, 128 * i : 128 * i + 128] = seq[128 * i : 128 * i + 128, :].T
    for n, rot in enumerate(ROT):
        for m in range(8):
            x = turned[16 * m : 16 * m + 16, :]
            if rot:
                x = pltpu.roll(x, SEQ - rot, 1)
            hi, lo = split(x[:, 0:K])
            hi_out[128 * n + 16 * m : 128 * n + 16 * m + 16, :] = hi
            lo_out[128 * n + 16 * m : 128 * n + 16 * m + 16, :] = lo


def main_kernel(me, q_in, lhs_hi, lhs_lo, out, rec, mag, seq, rhs_hi, rhs_lo, acc):
    for d in range(4):
        x = lax.rem(me[0] + 4 - d, 4)
        for high in range(2):
            for z in range(8):
                at = pl.multiple_of(((high * 8 + z) * 4) * TAU + x * TAU, 8)
                for pair in range(2):
                    rec[pair, pl.ds(at, TAU), :] = q_in[z, d, high, pair]
    normalize(rec, mag)
    seq[...] = jnp.zeros_like(seq)
    for pair in range(2):
        for i in range(12):
            x = rec[pair, 128 * i : 128 * i + 128, :]
            r32, r64, r96 = (pltpu.roll(x, n, 1) for n in (32, 64, 96))
            at = QFRONT + 2 * pair * ROW + 128 * i
            for e, parts in enumerate(((x, r32, r32, r64), (r64, r96, r96, x))):
                for n, part in enumerate(parts):
                    to = at + e * ROW - 8 * (n % 2)
                    seq[to : to + 128, 32 * n : 32 * n + 32] = part[:, 32 * n : 32 * n + 32]
    for k in range(K // CHUNK):
        for s in range(4):
            for m in range(CHUNK // 128):
                at = CHUNK * k + 128 * m
                hi, lo = split(seq[at + s : at + s + 128, :])
                rhs_hi[at : at + 128, 128 * s : 128 * s + 128] = hi
                rhs_lo[at : at + 128, 128 * s : 128 * s + 128] = lo
        span = slice(CHUNK * k, CHUNK * k + CHUNK)
        part = jnp.dot(lhs_hi[:, span], rhs_hi[span, :], preferred_element_type=jnp.float32)
        part += jnp.dot(lhs_hi[:, span], rhs_lo[span, :], preferred_element_type=jnp.float32)
        part += jnp.dot(lhs_lo[:, span], rhs_hi[span, :], preferred_element_type=jnp.float32)
        if k == 0:
            acc[...] = part
        else:
            acc[...] += part
    low = lanes((16, 128)) < 64
    for g in range(8):
        for x in range(4):
            at = 64 * g + 16 * x
            for s2 in range(2):
                a = acc[at : at + 16, 256 * s2 : 256 * s2 + 128]
                b = acc[at : at + 16, 256 * s2 + 128 : 256 * s2 + 256]
                out[0, x, g, s2] = jnp.where(low, a, pltpu.roll(b, 64, 1))
                out[1, x, g, s2] = jnp.where(low, pltpu.roll(a, 64, 1), b)


def final_kernel(got, out):
    lane = lanes((16, 128))
    for g in range(8):
        r, j = g // 2, g % 2
        r0, r1 = r % 2, r // 2
        for s2 in range(2):
            parts = [got[x, g, s2] for x in range(4)]
            for sb in range(2):
                for i in range(2):
                    mu = 2 * s2 + sb + 4 * (1 - r0) + 8 * i + 16 * (1 - j) + 32 * (1 - r1)
                    if mu == 0:
                        continue
                    n = 2 * sb + i
                    moved = [pltpu.roll(parts[x], (32 * (x - n)) % 128, 1) if x != n else parts[x] for x in range(4)]
                    value = jnp.where(lane < 32, moved[0], jnp.where(lane < 64, moved[1], jnp.where(lane < 96, moved[2], moved[3])))
                    out[:, mu - 1, :] = value * (1.0 / SAMPLES)


def sds(*shape, dtype=jnp.float32):
    return jax.ShapeDtypeStruct(shape, dtype)


def around(v, d):
    return lax.ppermute(v, "x", [(i, (i + d) % 4) for i in range(4)])


def local(raw):
    x = lax.axis_index("x")
    me = x.reshape(1).astype(jnp.int32)
    sent = pl.pallas_call(prepack, out_shape=sds(8, TAU, 768), in_specs=[VMEM], out_specs=VMEM, name="prepack")(raw[0])
    got = lax.all_to_all(sent, ("yh", "yl"), 0, 0, tiled=True)
    p_send, q_send = pl.pallas_call(
        repack, out_shape=(sds(8, 2, 2, TAU, 128), sds(4, 2, 2, TAU, 128)), in_specs=[VMEM], out_specs=(VMEM, VMEM), name="repack"
    )(got)
    p_mine = lax.all_to_all(p_send, "z", 0, 0, tiled=True)
    picked = [lax.dynamic_index_in_dim(q_send, lax.rem(x + d, 4), 0, keepdims=False) for d in range(4)]
    q_mine = jnp.stack([picked[0]] + [around(picked[d], d) for d in (1, 2, 3)])
    q_all = lax.all_to_all(jnp.broadcast_to(q_mine[None], (8,) + q_mine.shape), "z", 0, 0, tiled=True)
    p_all = [p_mine] + [around(p_mine, d) for d in (1, 2, 3)]
    lhs_hi, lhs_lo = pl.pallas_call(
        p_kernel,
        out_shape=(sds(512, K, dtype=jnp.bfloat16), sds(512, K, dtype=jnp.bfloat16)),
        in_specs=[SMEM] + [VMEM] * 4,
        out_specs=(VMEM, VMEM),
        scratch_shapes=[
            pltpu.VMEM((2, SAMPLES, 128), jnp.float32),
            pltpu.VMEM((SAMPLES + 2 * HALF, 256), jnp.bfloat16),
            pltpu.VMEM((SEQ, 128), jnp.float32),
            pltpu.VMEM((128, SEQ), jnp.float32),
        ],
        compiler_params=pltpu.CompilerParams(vmem_limit_bytes=BIG),
        cost_estimate=pl.CostEstimate(flops=10**9, bytes_accessed=20 * 10**6, transcendentals=0),
        name="p_side",
    )(me, *p_all)
    part = pl.pallas_call(
        main_kernel,
        out_shape=sds(2, 4, 8, 2, 16, 128),
        in_specs=[SMEM] + [VMEM] * 3,
        out_specs=VMEM,
        scratch_shapes=[
            pltpu.VMEM((2, SAMPLES, 128), jnp.float32),
            pltpu.VMEM((SAMPLES + 2 * HALF, 256), jnp.bfloat16),
            pltpu.VMEM((SEQ, 128), jnp.float32),
            pltpu.VMEM((K, 512), jnp.bfloat16),
            pltpu.VMEM((K, 512), jnp.bfloat16),
            pltpu.VMEM((512, 512), jnp.float32),
        ],
        compiler_params=pltpu.CompilerParams(vmem_limit_bytes=BIG),
        cost_estimate=pl.CostEstimate(flops=10**10, bytes_accessed=20 * 10**6, transcendentals=0),
        name="correlate",
    )(me, q_all, lhs_hi, lhs_lo)
    both = lax.all_to_all(part, "core", 0, 0, tiled=True)
    summed = both[0] + both[1]
    mine = lax.all_to_all(summed, "x", 0, 0, tiled=True)
    return pl.pallas_call(final_kernel, out_shape=sds(16, LAGS, 128), in_specs=[VMEM], out_specs=VMEM, name="finish")(mine)


def solution(mesh):
    grid = Mesh(mesh.devices.reshape(2, 8, 4, 4, 2), ("yh", "z", "x", "yl", "core"))
    in_specs = (P(("yl", "core"), ("yh", "z", "x"), None),)
    out_specs = P(("yh", "z", "x"), None, ("yl", "core"))
    return jax.shard_map(local, mesh=grid, in_specs=in_specs, out_specs=out_specs, check_vma=False)
```

```python
import functools

import jax
import jax.numpy as jnp
from jax import lax
from jax.experimental import pallas as pl
from jax.experimental.pallas import tpu as pltpu
from jax.sharding import Mesh, PartitionSpec as P

C = 1024
MAXLAG = 31
HALF = 64
LAGS = 63
SAMPLES = 1536
epsilon = 1e-06

TAU = 24
ROW = SAMPLES + 32
K = 3328
FRONT = 40
QFRONT = FRONT - 24
SEQ = K + 128
CHUNKS = (768, 768, 768, 1024)
ROT = (4, 8, 36, 40)
VMEM = pl.BlockSpec(memory_space=pltpu.VMEM)
SMEM = pl.BlockSpec(memory_space=pltpu.SMEM)
BIG = 34 * 1024 * 1024
SMALL = pltpu.CompilerParams(vmem_limit_bytes=8 * 1024 * 1024)


def lanes(shape):
    return lax.broadcasted_iota(jnp.int32, shape, len(shape) - 1)


def prepack(raw, out):
    lane = lanes((TAU, 128))
    for low in range(4):
        a = raw[:, 256 * low : 256 * low + 128]
        b = raw[:, 256 * low + 128 : 256 * low + 256]
        first = jnp.where(
            lane < 32, a, jnp.where(lane < 64, pltpu.roll(b, 32, 1), jnp.where(lane < 96, pltpu.roll(a, 32, 1), pltpu.roll(b, 64, 1)))
        )
        second = jnp.where(
            lane < 32, pltpu.roll(a, 64, 1), jnp.where(lane < 64, pltpu.roll(b, 96, 1), jnp.where(lane < 96, pltpu.roll(a, 96, 1), b))
        )
        for high in range(2):
            out[4 * high + low, :, 512:640] = first
            out[4 * high + low, :, 640:768] = second
            out[4 * high + low, :, 0:512] = raw[:, 512 * high : 512 * high + 512]


def repack(got, p_out, q_out):
    low = lanes((TAU, 128)) < 64
    for high in range(2):
        for pair in range(2):
            one, two = 4 * high + 2 * pair, 4 * high + 2 * pair + 1
            for v in range(6):
                a = got[one, :, 128 * v : 128 * v + 128]
                b = got[two, :, 128 * v : 128 * v + 128]
                even = jnp.where(low, a, pltpu.roll(b, 64, 1))
                odd = jnp.where(low, pltpu.roll(a, 64, 1), b)
                if v < 4:
                    p_out[2 * v, pair, high] = even
                    p_out[2 * v + 1, pair, high] = odd
                else:
                    q_out[pair, 2 * (v - 4), high] = even
                    q_out[pair, 2 * (v - 4) + 1, high] = odd


def split(x):
    hi = x.astype(jnp.bfloat16)
    return hi, (x - hi.astype(jnp.float32)).astype(jnp.bfloat16)


def normalize(rec, mag):
    row = lax.broadcasted_iota(jnp.int32, (128, 256), 0)
    col = lanes((128, 256))
    band = jnp.where((col >= row) & (col <= row + 2 * HALF), 1.0, 0.0).astype(jnp.bfloat16)
    zero = jnp.zeros((HALF, 256), jnp.bfloat16)
    mag[0:HALF, :] = zero
    mag[HALF + SAMPLES : 2 * HALF + SAMPLES, :] = zero
    for pair in range(2):
        mean = jnp.sum(rec[pair], axis=0, keepdims=True) * (1.0 / SAMPLES)
        for i in range(12):
            d = rec[pair, 128 * i : 128 * i + 128, :] - mean
            rec[pair, 128 * i : 128 * i + 128, :] = d
            hi, lo = split(jnp.abs(d))
            mag[HALF + 128 * i : HALF + 128 * i + 128, 0:128] = hi
            mag[HALF + 128 * i : HALF + 128 * i + 128, 128:256] = lo
        for i in range(12):
            both = jnp.dot(band, mag[128 * i : 128 * i + 256, :], preferred_element_type=jnp.float32)
            t = lax.broadcasted_iota(jnp.int32, (128, 128), 0) + 128 * i
            count = (jnp.minimum(t, HALF) + jnp.minimum(SAMPLES - 1 - t, HALF) + 1).astype(jnp.float32)
            running = (both[:, 0:128] + both[:, 128:256]) / count
            rec[pair, 128 * i : 128 * i + 128, :] = rec[pair, 128 * i : 128 * i + 128, :] / (running + epsilon)


def correlate(last, pair, me, p0, p1, p2, p3, q_in, *rest):
    if last:
        before, keep, send, *rest = rest
    else:
        total, *rest = rest
    rec, mag, pseq, qseq, turned, lhs_hi, lhs_lo, rhs_hi, rhs_lo = rest[:9]
    for d, ref in enumerate((p0, p1, p2, p3)):
        x = lax.rem(me[0] + 4 - d, 4)
        for high in range(2):
            for z in range(8):
                at = pl.multiple_of(((high * 8 + z) * 4) * TAU + x * TAU, 8)
                rec[0, pl.ds(at, TAU), :] = ref[z, pair, high]
                rec[1, pl.ds(at, TAU), :] = q_in[z, d, high]
    normalize(rec, mag)
    for seq in (pseq, qseq):
        seq[0:64, :] = jnp.zeros((64, 128), jnp.float32)
        at = QFRONT + SAMPLES - 16
        seq[at : at + 80, :] = jnp.zeros((80, 128), jnp.float32)
        at = QFRONT + ROW + SAMPLES - 16
        seq[at:SEQ, :] = jnp.zeros((SEQ - at, 128), jnp.float32)
    for i in range(12):
        x = rec[0, 128 * i : 128 * i + 128, :]
        r = pltpu.roll(x, 64, 1)
        at = FRONT + 128 * i
        pseq[at : at + 128, 0:64] = x[:, 0:64]
        pseq[at - 16 : at + 112, 64:128] = r[:, 64:128]
        at += ROW
        pseq[at : at + 128, 0:64] = r[:, 0:64]
        pseq[at - 16 : at + 112, 64:128] = x[:, 64:128]
        x = rec[1, 128 * i : 128 * i + 128, :]
        r32, r64, r96 = (pltpu.roll(x, n, 1) for n in (32, 64, 96))
        at = QFRONT + 128 * i
        for e, parts in enumerate(((x, r32, r32, r64), (r64, r96, r96, x))):
            for n, part in enumerate(parts):
                to = at + e * ROW - 8 * (n % 2)
                qseq[to : to + 128, 32 * n : 32 * n + 32] = part[:, 32 * n : 32 * n + 32]
    for i in range(SEQ // 128):
        turned[:, 128 * i : 128 * i + 128] = pseq[128 * i : 128 * i + 128, :].T
    acc = rest[9] if last else total
    start = 0
    for n, width in enumerate(CHUNKS):
        for m in range(8):
            wide = turned[16 * m : 16 * m + 16, start : start + width + 128]
            for r, rot in enumerate(ROT):
                hi, lo = split(pltpu.roll(wide, width + 128 - rot, 1)[:, 0:width])
                lhs_hi[128 * r + 16 * m : 128 * r + 16 * m + 16, start : start + width] = hi
                lhs_lo[128 * r + 16 * m : 128 * r + 16 * m + 16, start : start + width] = lo
        for s in range(4):
            for m in range(width // 128):
                at = start + 128 * m
                hi, lo = split(qseq[at + s : at + s + 128, :])
                rhs_hi[at : at + 128, 128 * s : 128 * s + 128] = hi
                rhs_lo[at : at + 128, 128 * s : 128 * s + 128] = lo
        span = slice(start, start + width)
        part = jnp.dot(lhs_hi[:, span], rhs_hi[span, :], preferred_element_type=jnp.float32)
        part += jnp.dot(lhs_hi[:, span], rhs_lo[span, :], preferred_element_type=jnp.float32)
        part += jnp.dot(lhs_lo[:, span], rhs_hi[span, :], preferred_element_type=jnp.float32)
        if n:
            acc[...] += part
        elif last:
            acc[...] = before[...] + part
        else:
            acc[...] = part
        start += width
    if not last:
        return
    low = lanes((16, 128)) < 64
    first = me[1] == 0
    for g in range(8):
        for x in range(4):
            at = 64 * g + 16 * x
            for s2 in range(2):
                a = acc[at : at + 16, 256 * s2 : 256 * s2 + 128]
                b = acc[at : at + 16, 256 * s2 + 128 : 256 * s2 + 256]
                one = jnp.where(low, a, pltpu.roll(b, 64, 1))
                two = jnp.where(low, pltpu.roll(a, 64, 1), b)
                keep[x, g, s2] = jnp.where(first, one, two)
                send[x, g, s2] = jnp.where(first, two, one)


def final_kernel(got, out):
    lane = lanes((16, 128))
    for g in range(8):
        r, j = g // 2, g % 2
        r0, r1 = r % 2, r // 2
        for s2 in range(2):
            parts = [got[x, g, s2] for x in range(4)]
            for sb in range(2):
                for i in range(2):
                    mu = 2 * s2 + sb + 4 * (1 - r0) + 8 * i + 16 * (1 - j) + 32 * (1 - r1)
                    if mu == 0:
                        continue
                    n = 2 * sb + i
                    moved = [pltpu.roll(parts[x], (32 * (x - n)) % 128, 1) if x != n else parts[x] for x in range(4)]
                    value = jnp.where(lane < 32, moved[0], jnp.where(lane < 64, moved[1], jnp.where(lane < 96, moved[2], moved[3])))
                    out[mu - 1] = value * (1.0 / SAMPLES)


def sds(*shape, dtype=jnp.float32):
    return jax.ShapeDtypeStruct(shape, dtype)


def around(v, d):
    return lax.ppermute(v, "x", [(i, (i + d) % 4) for i in range(4)])


def spread(v):
    return lax.all_to_all(jnp.broadcast_to(v[None], (8,) + v.shape), "z", 0, 0, tiled=True)


def local(raw):
    x = lax.axis_index("x")
    me = jnp.stack([x, lax.axis_index("core")]).astype(jnp.int32)
    sent = pl.pallas_call(prepack, out_shape=sds(8, TAU, 768), in_specs=[VMEM], out_specs=VMEM, compiler_params=SMALL, name="prepack")(raw[0])
    got = lax.all_to_all(sent, ("yh", "yl"), 0, 0, tiled=True)
    p_send, q_send = pl.pallas_call(
        repack, out_shape=(sds(8, 2, 2, TAU, 128), sds(2, 4, 2, TAU, 128)), in_specs=[VMEM], out_specs=(VMEM, VMEM), compiler_params=SMALL, name="repack"
    )(got)
    p_mine = lax.all_to_all(p_send, "z", 0, 0, tiled=True)
    picked = [lax.dynamic_index_in_dim(q_send, lax.rem(x + d, 4), 1, keepdims=False) for d in range(4)]
    q_mine = [picked[0]] + [around(picked[d], d) for d in (1, 2, 3)]
    first = jnp.stack([q[0] for q in q_mine])
    second = jnp.stack([q[1] for q in q_mine])
    q_all = [spread(first)]
    second, *p_all = lax.optimization_barrier((second, p_mine, *(around(p_mine, d) for d in (1, 2, 3))))
    q_all.append(spread(second))
    scratch = [
        pltpu.VMEM((2, SAMPLES, 128), jnp.float32),
        pltpu.VMEM((SAMPLES + 2 * HALF, 256), jnp.bfloat16),
        pltpu.VMEM((SEQ, 128), jnp.float32),
        pltpu.VMEM((SEQ, 128), jnp.float32),
        pltpu.VMEM((128, SEQ), jnp.float32),
        pltpu.VMEM((512, K), jnp.bfloat16),
        pltpu.VMEM((512, K), jnp.bfloat16),
        pltpu.VMEM((K, 512), jnp.bfloat16),
        pltpu.VMEM((K, 512), jnp.bfloat16),
    ]
    params = pltpu.CompilerParams(vmem_limit_bytes=BIG)
    cost = pl.CostEstimate(flops=5 * 10**9, bytes_accessed=4 * 10**6, transcendentals=0)
    total = pl.pallas_call(
        functools.partial(correlate, False, 0),
        out_shape=sds(512, 512),
        in_specs=[SMEM] + [VMEM] * 5,
        out_specs=VMEM,
        scratch_shapes=scratch,
        compiler_params=params,
        cost_estimate=cost,
        name="first_pair",
    )(me, *p_all, q_all[0])
    keep, send = pl.pallas_call(
        functools.partial(correlate, True, 1),
        out_shape=(sds(4, 8, 2, 16, 128), sds(4, 8, 2, 16, 128)),
        in_specs=[SMEM] + [VMEM] * 6,
        out_specs=(VMEM, VMEM),
        scratch_shapes=scratch + [pltpu.VMEM((512, 512), jnp.float32)],
        compiler_params=params,
        cost_estimate=cost,
        name="second_pair",
    )(me, *p_all, q_all[1], total)
    summed = keep + lax.ppermute(send, "core", [(0, 1), (1, 0)])
    mine = lax.all_to_all(summed, "x", 0, 0, tiled=True)
    out = pl.pallas_call(final_kernel, out_shape=sds(LAGS, 16, 128), in_specs=[VMEM], out_specs=VMEM, compiler_params=SMALL, name="finish")(mine)
    return jnp.transpose(out, (1, 0, 2))


def solution(mesh):
    grid = Mesh(mesh.devices.reshape(2, 8, 4, 4, 2), ("yh", "z", "x", "yl", "core"))
    in_specs = (P(("yl", "core"), ("yh", "z", "x"), None),)
    out_specs = P(("yh", "z", "x"), None, ("yl", "core"))
    return jax.shard_map(local, mesh=grid, in_specs=in_specs, out_specs=out_specs, check_vma=False)
```

```python
import functools

import jax
import jax.numpy as jnp
from jax import lax
from jax.experimental import pallas as pl
from jax.experimental.pallas import tpu as pltpu
from jax.sharding import Mesh, PartitionSpec as P

C = 1024
MAXLAG = 31
HALF = 64
LAGS = 63
SAMPLES = 1536
epsilon = 1e-06

TAU = 24
ROW = SAMPLES + 32
K = 3328
FRONT = 40
QFRONT = FRONT - 24
SEQ = K + 128
CHUNKS = (768, 768, 768, 1024)
ROT = (4, 8, 36, 40)
VMEM = pl.BlockSpec(memory_space=pltpu.VMEM)
SMEM = pl.BlockSpec(memory_space=pltpu.SMEM)
BIG = 34 * 1024 * 1024
SMALL = pltpu.CompilerParams(vmem_limit_bytes=8 * 1024 * 1024)


def lanes(shape):
    return lax.broadcasted_iota(jnp.int32, shape, len(shape) - 1)


def prepack(raw, out):
    lane = lanes((TAU, 128))
    for low in range(4):
        a = raw[:, 256 * low : 256 * low + 128]
        b = raw[:, 256 * low + 128 : 256 * low + 256]
        first = jnp.where(
            lane < 32, a, jnp.where(lane < 64, pltpu.roll(b, 32, 1), jnp.where(lane < 96, pltpu.roll(a, 32, 1), pltpu.roll(b, 64, 1)))
        )
        second = jnp.where(
            lane < 32, pltpu.roll(a, 64, 1), jnp.where(lane < 64, pltpu.roll(b, 96, 1), jnp.where(lane < 96, pltpu.roll(a, 96, 1), b))
        )
        for high in range(2):
            out[4 * high + low, :, 512:640] = first
            out[4 * high + low, :, 640:768] = second
            out[4 * high + low, :, 0:512] = raw[:, 512 * high : 512 * high + 512]


def pairs(got, high, pair, at):
    low = lanes((TAU, 128)) < 64
    a = got[4 * high + 2 * pair, :, at : at + 128]
    b = got[4 * high + 2 * pair + 1, :, at : at + 128]
    return jnp.where(low, a, pltpu.roll(b, 64, 1)), jnp.where(low, pltpu.roll(a, 64, 1), b)


def repack_p(got, out, rest):
    for high in range(2):
        for pair in range(2):
            for v in range(4):
                out[2 * v, pair, high], out[2 * v + 1, pair, high] = pairs(got, high, pair, 128 * v)
    rest[...] = got[:, :, 512:768]


def repack_q(me, got, out):
    for high in range(2):
        for pair in range(2):
            for v in range(2):
                for n, block in enumerate(pairs(got, high, pair, 128 * v)):
                    out[lax.rem(2 * v + n + 4 - me[0], 4), pair, high] = block


def split(x):
    hi = x.astype(jnp.bfloat16)
    return hi, (x - hi.astype(jnp.float32)).astype(jnp.bfloat16)


def normalize(rec, mag):
    row = lax.broadcasted_iota(jnp.int32, (128, 256), 0)
    col = lanes((128, 256))
    band = jnp.where((col >= row) & (col <= row + 2 * HALF), 1.0, 0.0).astype(jnp.bfloat16)
    zero = jnp.zeros((HALF, 256), jnp.bfloat16)
    mag[0:HALF, :] = zero
    mag[HALF + SAMPLES : 2 * HALF + SAMPLES, :] = zero
    for pair in range(2):
        mean = jnp.sum(rec[pair], axis=0, keepdims=True) * (1.0 / SAMPLES)
        for i in range(12):
            d = rec[pair, 128 * i : 128 * i + 128, :] - mean
            rec[pair, 128 * i : 128 * i + 128, :] = d
            hi, lo = split(jnp.abs(d))
            mag[HALF + 128 * i : HALF + 128 * i + 128, 0:128] = hi
            mag[HALF + 128 * i : HALF + 128 * i + 128, 128:256] = lo
        for i in range(12):
            both = jnp.dot(band, mag[128 * i : 128 * i + 256, :], preferred_element_type=jnp.float32)
            t = lax.broadcasted_iota(jnp.int32, (128, 128), 0) + 128 * i
            count = (jnp.minimum(t, HALF) + jnp.minimum(SAMPLES - 1 - t, HALF) + 1).astype(jnp.float32)
            running = (both[:, 0:128] + both[:, 128:256]) / count
            rec[pair, 128 * i : 128 * i + 128, :] = rec[pair, 128 * i : 128 * i + 128, :] / (running + epsilon)


def correlate(last, me, p0, p1, p2, p3, q_in, *rest):
    if last:
        before, keep, send, *rest = rest
    else:
        total, *rest = rest
    rec, mag, pseq, qseq, turned, lhs_hi, lhs_lo, rhs_hi, rhs_lo = rest[:9]
    for d, ref in enumerate((p0, p1, p2, p3)):
        x = lax.rem(me[0] + 4 - d, 4)
        for high in range(2):
            for z in range(8):
                at = pl.multiple_of(((high * 8 + z) * 4) * TAU + x * TAU, 8)
                rec[0, pl.ds(at, TAU), :] = ref[z, high]
                rec[1, pl.ds(at, TAU), :] = q_in[z, d, high]
    normalize(rec, mag)
    for seq in (pseq, qseq):
        seq[0:64, :] = jnp.zeros((64, 128), jnp.float32)
        at = QFRONT + SAMPLES - 16
        seq[at : at + 80, :] = jnp.zeros((80, 128), jnp.float32)
        at = QFRONT + ROW + SAMPLES - 16
        seq[at:SEQ, :] = jnp.zeros((SEQ - at, 128), jnp.float32)
    for i in range(12):
        x = rec[0, 128 * i : 128 * i + 128, :]
        r = pltpu.roll(x, 64, 1)
        at = FRONT + 128 * i
        pseq[at : at + 128, 0:64] = x[:, 0:64]
        pseq[at - 16 : at + 112, 64:128] = r[:, 64:128]
        at += ROW
        pseq[at : at + 128, 0:64] = r[:, 0:64]
        pseq[at - 16 : at + 112, 64:128] = x[:, 64:128]
        x = rec[1, 128 * i : 128 * i + 128, :]
        r32, r64, r96 = (pltpu.roll(x, n, 1) for n in (32, 64, 96))
        at = QFRONT + 128 * i
        for e, parts in enumerate(((x, r32, r32, r64), (r64, r96, r96, x))):
            for n, part in enumerate(parts):
                to = at + e * ROW - 8 * (n % 2)
                qseq[to : to + 128, 32 * n : 32 * n + 32] = part[:, 32 * n : 32 * n + 32]
    for i in range(SEQ // 128):
        turned[:, 128 * i : 128 * i + 128] = pseq[128 * i : 128 * i + 128, :].T
    acc = rest[9] if last else total
    start = 0
    for n, width in enumerate(CHUNKS):
        for m in range(8):
            wide = turned[16 * m : 16 * m + 16, start : start + width + 128]
            for r, rot in enumerate(ROT):
                hi, lo = split(pltpu.roll(wide, width + 128 - rot, 1)[:, 0:width])
                lhs_hi[128 * r + 16 * m : 128 * r + 16 * m + 16, start : start + width] = hi
                lhs_lo[128 * r + 16 * m : 128 * r + 16 * m + 16, start : start + width] = lo
        for s in range(4):
            for m in range(width // 128):
                at = start + 128 * m
                hi, lo = split(qseq[at + s : at + s + 128, :])
                rhs_hi[at : at + 128, 128 * s : 128 * s + 128] = hi
                rhs_lo[at : at + 128, 128 * s : 128 * s + 128] = lo
        span = slice(start, start + width)
        part = jnp.dot(lhs_hi[:, span], rhs_hi[span, :], preferred_element_type=jnp.float32)
        part += jnp.dot(lhs_hi[:, span], rhs_lo[span, :], preferred_element_type=jnp.float32)
        part += jnp.dot(lhs_lo[:, span], rhs_hi[span, :], preferred_element_type=jnp.float32)
        if n:
            acc[...] += part
        elif last:
            acc[...] = before[...] + part
        else:
            acc[...] = part
        start += width
    if not last:
        return
    low = lanes((16, 128)) < 64
    first = me[1] == 0
    for g in range(8):
        for x in range(4):
            at = 64 * g + 16 * x
            for s2 in range(2):
                a = acc[at : at + 16, 256 * s2 : 256 * s2 + 128]
                b = acc[at : at + 16, 256 * s2 + 128 : 256 * s2 + 256]
                one = jnp.where(low, a, pltpu.roll(b, 64, 1))
                two = jnp.where(low, pltpu.roll(a, 64, 1), b)
                keep[x, g, s2] = jnp.where(first, one, two)
                send[x, g, s2] = jnp.where(first, two, one)


def final_kernel(got, out):
    lane = lanes((16, 128))
    for g in range(8):
        r, j = g // 2, g % 2
        r0, r1 = r % 2, r // 2
        for s2 in range(2):
            parts = [got[x, g, s2] for x in range(4)]
            for sb in range(2):
                for i in range(2):
                    mu = 2 * s2 + sb + 4 * (1 - r0) + 8 * i + 16 * (1 - j) + 32 * (1 - r1)
                    if mu == 0:
                        continue
                    n = 2 * sb + i
                    moved = [pltpu.roll(parts[x], (32 * (x - n)) % 128, 1) if x != n else parts[x] for x in range(4)]
                    value = jnp.where(lane < 32, moved[0], jnp.where(lane < 64, moved[1], jnp.where(lane < 96, moved[2], moved[3])))
                    out[mu - 1] = value * (1.0 / SAMPLES)


def sds(*shape, dtype=jnp.float32):
    return jax.ShapeDtypeStruct(shape, dtype)


def around(v, d):
    return lax.ppermute(v, "x", [(i, (i + d) % 4) for i in range(4)])


def copies(v):
    return jnp.broadcast_to(v[None], (8,) + v.shape)


def to_all(v):
    return lax.all_to_all(v, "z", 0, 0, tiled=True)


def local(raw):
    x = lax.axis_index("x")
    me = jnp.stack([x, lax.axis_index("core")]).astype(jnp.int32)
    sent = pl.pallas_call(prepack, out_shape=sds(8, TAU, 768), in_specs=[VMEM], out_specs=VMEM, compiler_params=SMALL, name="prepack")(raw[0])
    got = lax.all_to_all(sent, ("yh", "yl"), 0, 0, tiled=True)
    p_send, rest = pl.pallas_call(
        repack_p,
        out_shape=(sds(8, 2, 2, TAU, 128), sds(8, TAU, 256)),
        in_specs=[VMEM],
        out_specs=(VMEM, VMEM),
        compiler_params=SMALL,
        name="repack_p",
    )(got)
    p_mine = to_all(p_send)
    q_send = pl.pallas_call(
        repack_q,
        out_shape=sds(4, 2, 2, TAU, 128),
        in_specs=[SMEM, VMEM],
        out_specs=VMEM,
        compiler_params=SMALL,
        cost_estimate=pl.CostEstimate(flops=0, bytes_accessed=6 * 10**7, transcendentals=0),
        name="repack_q",
    )(me, rest)
    q_mine = [q_send[0]] + [around(q_send[d], d) for d in (1, 2, 3)]
    first = jnp.stack([q[0] for q in q_mine])
    second = copies(jnp.stack([q[1] for q in q_mine]))
    p_first, p_second = p_mine[:, 0], p_mine[:, 1]
    q_first = to_all(copies(first))
    second, *p_first = lax.optimization_barrier((second, p_first, *(around(p_first, d) for d in (1, 2, 3))))
    q_second = to_all(second)
    p_second, q_first = lax.optimization_barrier((p_second, q_first))
    p_second = [p_second] + [around(p_second, d) for d in (1, 2, 3)]
    scratch = [
        pltpu.VMEM((2, SAMPLES, 128), jnp.float32),
        pltpu.VMEM((SAMPLES + 2 * HALF, 256), jnp.bfloat16),
        pltpu.VMEM((SEQ, 128), jnp.float32),
        pltpu.VMEM((SEQ, 128), jnp.float32),
        pltpu.VMEM((128, SEQ), jnp.float32),
        pltpu.VMEM((512, K), jnp.bfloat16),
        pltpu.VMEM((512, K), jnp.bfloat16),
        pltpu.VMEM((K, 512), jnp.bfloat16),
        pltpu.VMEM((K, 512), jnp.bfloat16),
    ]
    params = pltpu.CompilerParams(vmem_limit_bytes=BIG)
    cost = pl.CostEstimate(flops=5 * 10**9, bytes_accessed=4 * 10**6, transcendentals=0)
    total = pl.pallas_call(
        functools.partial(correlate, False),
        out_shape=sds(512, 512),
        in_specs=[SMEM] + [VMEM] * 5,
        out_specs=VMEM,
        scratch_shapes=scratch,
        compiler_params=params,
        cost_estimate=cost,
        name="first_pair",
    )(me, *p_first, q_first)
    keep, send = pl.pallas_call(
        functools.partial(correlate, True),
        out_shape=(sds(4, 8, 2, 16, 128), sds(4, 8, 2, 16, 128)),
        in_specs=[SMEM] + [VMEM] * 6,
        out_specs=(VMEM, VMEM),
        scratch_shapes=scratch + [pltpu.VMEM((512, 512), jnp.float32)],
        compiler_params=params,
        cost_estimate=cost,
        name="second_pair",
    )(me, *p_second, q_second, total)
    summed = keep + lax.ppermute(send, "core", [(0, 1), (1, 0)])
    mine = lax.all_to_all(summed, "x", 0, 0, tiled=True)
    out = pl.pallas_call(final_kernel, out_shape=sds(LAGS, 16, 128), in_specs=[VMEM], out_specs=VMEM, compiler_params=SMALL, name="finish")(mine)
    return jnp.transpose(out, (1, 0, 2))


def solution(mesh):
    grid = Mesh(mesh.devices.reshape(2, 8, 4, 4, 2), ("yh", "z", "x", "yl", "core"))
    in_specs = (P(("yl", "core"), ("yh", "z", "x"), None),)
    out_specs = P(("yh", "z", "x"), None, ("yl", "core"))
    return jax.shard_map(local, mesh=grid, in_specs=in_specs, out_specs=out_specs, check_vma=False)
```

```python
import functools

import jax
import jax.numpy as jnp
from jax import lax
from jax.experimental import pallas as pl
from jax.experimental.pallas import tpu as pltpu
from jax.sharding import Mesh, PartitionSpec as P

C = 1024
MAXLAG = 31
HALF = 64
LAGS = 63
SAMPLES = 1536
epsilon = 1e-06

TAU = 24
ROW = SAMPLES + 32
K = 3328
FRONT = 40
QFRONT = FRONT - 24
SEQ = K + 128
CHUNKS = (768, 768, 768, 1024)
ROT = (4, 8, 36, 40)
VMEM = pl.BlockSpec(memory_space=pltpu.VMEM)
SMEM = pl.BlockSpec(memory_space=pltpu.SMEM)
BIG = 34 * 1024 * 1024
SMALL = pltpu.CompilerParams(vmem_limit_bytes=8 * 1024 * 1024)


def lanes(shape):
    return lax.broadcasted_iota(jnp.int32, shape, len(shape) - 1)


def prepack(raw, out):
    lane = lanes((TAU, 128))
    for low in range(4):
        a = raw[:, 256 * low : 256 * low + 128]
        b = raw[:, 256 * low + 128 : 256 * low + 256]
        first = jnp.where(
            lane < 32, a, jnp.where(lane < 64, pltpu.roll(b, 32, 1), jnp.where(lane < 96, pltpu.roll(a, 32, 1), pltpu.roll(b, 64, 1)))
        )
        second = jnp.where(
            lane < 32, pltpu.roll(a, 64, 1), jnp.where(lane < 64, pltpu.roll(b, 96, 1), jnp.where(lane < 96, pltpu.roll(a, 96, 1), b))
        )
        for high in range(2):
            out[4 * high + low, :, 512:640] = first
            out[4 * high + low, :, 640:768] = second
            out[4 * high + low, :, 0:512] = raw[:, 512 * high : 512 * high + 512]


def pairs(got, high, pair, at):
    low = lanes((TAU, 128)) < 64
    a = got[4 * high + 2 * pair, :, at : at + 128]
    b = got[4 * high + 2 * pair + 1, :, at : at + 128]
    return jnp.where(low, a, pltpu.roll(b, 64, 1)), jnp.where(low, pltpu.roll(a, 64, 1), b)


def repack_p(got, out, rest):
    for high in range(2):
        for pair in range(2):
            for v in range(4):
                out[2 * v, pair, high], out[2 * v + 1, pair, high] = pairs(got, high, pair, 128 * v)
    rest[...] = got[:, :, 512:768]


def repack_q(me, got, out):
    for high in range(2):
        for pair in range(2):
            for v in range(2):
                for n, block in enumerate(pairs(got, high, pair, 128 * v)):
                    out[lax.rem(2 * v + n + 4 - me[0], 4), pair, high] = block


def split(x):
    hi = x.astype(jnp.bfloat16)
    return hi, (x - hi.astype(jnp.float32)).astype(jnp.bfloat16)


def normalize(rec, mag):
    row = lax.broadcasted_iota(jnp.int32, (128, 256), 0)
    col = lanes((128, 256))
    band = jnp.where((col >= row) & (col <= row + 2 * HALF), 1.0, 0.0).astype(jnp.bfloat16)
    zero = jnp.zeros((HALF, 256), jnp.bfloat16)
    mag[0:HALF, :] = zero
    mag[HALF + SAMPLES : 2 * HALF + SAMPLES, :] = zero
    for pair in range(2):
        mean = jnp.sum(rec[pair], axis=0, keepdims=True) * (1.0 / SAMPLES)
        for i in range(12):
            d = rec[pair, 128 * i : 128 * i + 128, :] - mean
            rec[pair, 128 * i : 128 * i + 128, :] = d
            hi, lo = split(jnp.abs(d))
            mag[HALF + 128 * i : HALF + 128 * i + 128, 0:128] = hi
            mag[HALF + 128 * i : HALF + 128 * i + 128, 128:256] = lo
        for i in range(12):
            both = jnp.dot(band, mag[128 * i : 128 * i + 256, :], preferred_element_type=jnp.float32)
            t = lax.broadcasted_iota(jnp.int32, (128, 128), 0) + 128 * i
            count = (jnp.minimum(t, HALF) + jnp.minimum(SAMPLES - 1 - t, HALF) + 1).astype(jnp.float32)
            running = (both[:, 0:128] + both[:, 128:256]) / count
            rec[pair, 128 * i : 128 * i + 128, :] = rec[pair, 128 * i : 128 * i + 128, :] / (running + epsilon)


def correlate(last, me, p0, p1, p2, p3, q_in, *rest):
    if last:
        before, keep, send, *rest = rest
    else:
        total, *rest = rest
    rec, mag, pseq, qseq, turned, lhs_hi, lhs_lo, rhs_hi, rhs_lo = rest[:9]
    for d, ref in enumerate((p0, p1, p2, p3)):
        x = lax.rem(me[0] + 4 - d, 4)
        for high in range(2):
            for z in range(8):
                at = pl.multiple_of(((high * 8 + z) * 4) * TAU + x * TAU, 8)
                rec[0, pl.ds(at, TAU), :] = ref[z, high]
                rec[1, pl.ds(at, TAU), :] = q_in[z, d, high]
    normalize(rec, mag)
    for seq in (pseq, qseq):
        seq[0:64, :] = jnp.zeros((64, 128), jnp.float32)
        at = QFRONT + SAMPLES - 16
        seq[at : at + 80, :] = jnp.zeros((80, 128), jnp.float32)
        at = QFRONT + ROW + SAMPLES - 16
        seq[at:SEQ, :] = jnp.zeros((SEQ - at, 128), jnp.float32)
    for i in range(12):
        x = rec[0, 128 * i : 128 * i + 128, :]
        r = pltpu.roll(x, 64, 1)
        at = FRONT + 128 * i
        pseq[at : at + 128, 0:64] = x[:, 0:64]
        pseq[at - 16 : at + 112, 64:128] = r[:, 64:128]
        at += ROW
        pseq[at : at + 128, 0:64] = r[:, 0:64]
        pseq[at - 16 : at + 112, 64:128] = x[:, 64:128]
        x = rec[1, 128 * i : 128 * i + 128, :]
        r32, r64, r96 = (pltpu.roll(x, n, 1) for n in (32, 64, 96))
        at = QFRONT + 128 * i
        for e, parts in enumerate(((x, r32, r32, r64), (r64, r96, r96, x))):
            for n, part in enumerate(parts):
                to = at + e * ROW - 8 * (n % 2)
                qseq[to : to + 128, 32 * n : 32 * n + 32] = part[:, 32 * n : 32 * n + 32]
    for i in range(SEQ // 128):
        turned[:, 128 * i : 128 * i + 128] = pseq[128 * i : 128 * i + 128, :].T
    acc = rest[9] if last else total
    start = 0
    for n, width in enumerate(CHUNKS):
        for m in range(8):
            wide = turned[16 * m : 16 * m + 16, start : start + width + 128]
            for r, rot in enumerate(ROT):
                hi, lo = split(pltpu.roll(wide, width + 128 - rot, 1)[:, 0:width])
                lhs_hi[128 * r + 16 * m : 128 * r + 16 * m + 16, start : start + width] = hi
                lhs_lo[128 * r + 16 * m : 128 * r + 16 * m + 16, start : start + width] = lo
        for s in range(4):
            for m in range(width // 128):
                at = start + 128 * m
                hi, lo = split(qseq[at + s : at + s + 128, :])
                rhs_hi[at : at + 128, 128 * s : 128 * s + 128] = hi
                rhs_lo[at : at + 128, 128 * s : 128 * s + 128] = lo
        span = slice(start, start + width)
        part = jnp.dot(lhs_hi[:, span], rhs_hi[span, :], preferred_element_type=jnp.float32)
        part += jnp.dot(lhs_hi[:, span], rhs_lo[span, :], preferred_element_type=jnp.float32)
        part += jnp.dot(lhs_lo[:, span], rhs_hi[span, :], preferred_element_type=jnp.float32)
        if n:
            acc[...] += part
        elif last:
            acc[...] = before[...] + part
        else:
            acc[...] = part
        start += width
    if not last:
        return
    low = lanes((16, 128)) < 64
    first = me[1] == 0
    for g in range(8):
        for x in range(4):
            at = 64 * g + 16 * x
            for s2 in range(2):
                a = acc[at : at + 16, 256 * s2 : 256 * s2 + 128]
                b = acc[at : at + 16, 256 * s2 + 128 : 256 * s2 + 256]
                one = jnp.where(low, a, pltpu.roll(b, 64, 1))
                two = jnp.where(low, pltpu.roll(a, 64, 1), b)
                keep[x, g, s2] = jnp.where(first, one, two)
                send[x, g, s2] = jnp.where(first, two, one)


def final_kernel(got, out):
    lane = lanes((16, 128))
    for g in range(8):
        r, j = g // 2, g % 2
        r0, r1 = r % 2, r // 2
        for s2 in range(2):
            parts = [got[x, g, s2] for x in range(4)]
            for sb in range(2):
                for i in range(2):
                    mu = 2 * s2 + sb + 4 * (1 - r0) + 8 * i + 16 * (1 - j) + 32 * (1 - r1)
                    if mu == 0:
                        continue
                    n = 2 * sb + i
                    moved = [pltpu.roll(parts[x], (32 * (x - n)) % 128, 1) if x != n else parts[x] for x in range(4)]
                    value = jnp.where(lane < 32, moved[0], jnp.where(lane < 64, moved[1], jnp.where(lane < 96, moved[2], moved[3])))
                    out[mu - 1] = value * (1.0 / SAMPLES)


def sds(*shape, dtype=jnp.float32):
    return jax.ShapeDtypeStruct(shape, dtype)


def around(v, d):
    return lax.ppermute(v, "x", [(i, (i + d) % 4) for i in range(4)])


def copies(v):
    return jnp.broadcast_to(v[None], (8,) + v.shape)


def to_all(v):
    return lax.all_to_all(v, "z", 0, 0, tiled=True)


def local(raw):
    x = lax.axis_index("x")
    me = jnp.stack([x, lax.axis_index("core")]).astype(jnp.int32)
    sent = pl.pallas_call(prepack, out_shape=sds(8, TAU, 768), in_specs=[VMEM], out_specs=VMEM, compiler_params=SMALL, name="prepack")(raw[0])
    got = lax.all_to_all(sent, ("yh", "yl"), 0, 0, tiled=True)
    p_send, rest = pl.pallas_call(
        repack_p,
        out_shape=(sds(8, 2, 2, TAU, 128), sds(8, TAU, 256)),
        in_specs=[VMEM],
        out_specs=(VMEM, VMEM),
        compiler_params=SMALL,
        name="repack_p",
    )(got)
    p_mine = to_all(p_send)
    q_send = pl.pallas_call(
        repack_q,
        out_shape=sds(4, 2, 2, TAU, 128),
        in_specs=[SMEM, VMEM],
        out_specs=VMEM,
        compiler_params=SMALL,
        cost_estimate=pl.CostEstimate(flops=0, bytes_accessed=6 * 10**7, transcendentals=0),
        name="repack_q",
    )(me, rest)
    q_mine = [q_send[0]] + [around(q_send[d], d) for d in (1, 2, 3)]
    p_mine, *q_mine = lax.optimization_barrier((p_mine, *q_mine))
    first = jnp.stack([q[0] for q in q_mine])
    second = copies(jnp.stack([q[1] for q in q_mine]))
    p_first, p_second = p_mine[:, 0], p_mine[:, 1]
    q_first = to_all(copies(first))
    second, p_second, *p_first = lax.optimization_barrier((second, p_second, p_first, *(around(p_first, d) for d in (1, 2, 3))))
    q_second = to_all(second)
    p_second = [p_second] + [around(p_second, d) for d in (1, 2, 3)]
    scratch = [
        pltpu.VMEM((2, SAMPLES, 128), jnp.float32),
        pltpu.VMEM((SAMPLES + 2 * HALF, 256), jnp.bfloat16),
        pltpu.VMEM((SEQ, 128), jnp.float32),
        pltpu.VMEM((SEQ, 128), jnp.float32),
        pltpu.VMEM((128, SEQ), jnp.float32),
        pltpu.VMEM((512, K), jnp.bfloat16),
        pltpu.VMEM((512, K), jnp.bfloat16),
        pltpu.VMEM((K, 512), jnp.bfloat16),
        pltpu.VMEM((K, 512), jnp.bfloat16),
    ]
    params = pltpu.CompilerParams(vmem_limit_bytes=BIG)
    cost = pl.CostEstimate(flops=5 * 10**9, bytes_accessed=4 * 10**6, transcendentals=0)
    total = pl.pallas_call(
        functools.partial(correlate, False),
        out_shape=sds(512, 512),
        in_specs=[SMEM] + [VMEM] * 5,
        out_specs=VMEM,
        scratch_shapes=scratch,
        compiler_params=params,
        cost_estimate=cost,
        name="first_pair",
    )(me, *p_first, q_first)
    keep, send = pl.pallas_call(
        functools.partial(correlate, True),
        out_shape=(sds(4, 8, 2, 16, 128), sds(4, 8, 2, 16, 128)),
        in_specs=[SMEM] + [VMEM] * 6,
        out_specs=(VMEM, VMEM),
        scratch_shapes=scratch + [pltpu.VMEM((512, 512), jnp.float32)],
        compiler_params=params,
        cost_estimate=cost,
        name="second_pair",
    )(me, *p_second, q_second, total)
    summed = keep + lax.ppermute(send, "core", [(0, 1), (1, 0)])
    mine = lax.all_to_all(summed, "x", 0, 0, tiled=True)
    out = pl.pallas_call(final_kernel, out_shape=sds(LAGS, 16, 128), in_specs=[VMEM], out_specs=VMEM, compiler_params=SMALL, name="finish")(mine)
    return jnp.transpose(out, (1, 0, 2))


def solution(mesh):
    grid = Mesh(mesh.devices.reshape(2, 8, 4, 4, 2), ("yh", "z", "x", "yl", "core"))
    in_specs = (P(("yl", "core"), ("yh", "z", "x"), None),)
    out_specs = P(("yh", "z", "x"), None, ("yl", "core"))
    return jax.shard_map(local, mesh=grid, in_specs=in_specs, out_specs=out_specs, check_vma=False)
```

```python
import jax
import jax.numpy as jnp
from jax import lax
from jax.experimental import pallas as pl
from jax.experimental.pallas import tpu as pltpu
from jax.sharding import Mesh, PartitionSpec as P

C = 1024
MAXLAG = 31
HALF = 64
LAGS = 63
SAMPLES = 1536
epsilon = 1e-06

TAU = 24
ROW = SAMPLES + 32
K = 3328
FRONT = 40
QFRONT = FRONT - 24
SEQ = K + 128
CHUNKS = (768, 768, 768, 1024)
WIDE = 256
ROT = (4, 8, 36, 40)
VMEM = pl.BlockSpec(memory_space=pltpu.VMEM)
HBM = pl.BlockSpec(memory_space=pltpu.HBM)
SMEM = pl.BlockSpec(memory_space=pltpu.SMEM)
P_VMEM = 49 * 1024 * 1024
Q_VMEM = 49 * 1024 * 1024
SMALL = pltpu.CompilerParams(vmem_limit_bytes=8 * 1024 * 1024)


def lanes(shape):
    return lax.broadcasted_iota(jnp.int32, shape, len(shape) - 1)


def prepack(raw, out):
    lane = lanes((TAU, 128))
    for low in range(4):
        a = raw[:, 256 * low : 256 * low + 128]
        b = raw[:, 256 * low + 128 : 256 * low + 256]
        first = jnp.where(
            lane < 32, a, jnp.where(lane < 64, pltpu.roll(b, 32, 1), jnp.where(lane < 96, pltpu.roll(a, 32, 1), pltpu.roll(b, 64, 1)))
        )
        second = jnp.where(
            lane < 32, pltpu.roll(a, 64, 1), jnp.where(lane < 64, pltpu.roll(b, 96, 1), jnp.where(lane < 96, pltpu.roll(a, 96, 1), b))
        )
        for high in range(2):
            out[4 * high + low, :, 512:640] = first
            out[4 * high + low, :, 640:768] = second
            out[4 * high + low, :, 0:512] = raw[:, 512 * high : 512 * high + 512]


def pairs(got, high, pair, at):
    low = lanes((TAU, 128)) < 64
    a = got[4 * high + 2 * pair, :, at : at + 128]
    b = got[4 * high + 2 * pair + 1, :, at : at + 128]
    return jnp.where(low, a, pltpu.roll(b, 64, 1)), jnp.where(low, pltpu.roll(a, 64, 1), b)


def repack_p(got, out, rest):
    for high in range(2):
        for pair in range(2):
            for v in range(4):
                out[2 * v, pair, high], out[2 * v + 1, pair, high] = pairs(got, high, pair, 128 * v)
    rest[...] = got[:, :, 512:768]


def repack_q(me, got, out):
    for high in range(2):
        for pair in range(2):
            for v in range(2):
                for n, block in enumerate(pairs(got, high, pair, 128 * v)):
                    out[lax.rem(2 * v + n + 4 - me[0], 4), pair, high] = block


def split(x):
    hi = x.astype(jnp.bfloat16)
    return hi, (x - hi.astype(jnp.float32)).astype(jnp.bfloat16)


def normalize(rec, mag):
    row = lax.broadcasted_iota(jnp.int32, (128, 256), 0)
    col = lanes((128, 256))
    band = jnp.where((col >= row) & (col <= row + 2 * HALF), 1.0, 0.0).astype(jnp.bfloat16)
    zero = jnp.zeros((HALF, 256), jnp.bfloat16)
    mag[0:HALF, :] = zero
    mag[HALF + SAMPLES : 2 * HALF + SAMPLES, :] = zero
    for pair in range(2):
        mean = jnp.sum(rec[pair], axis=0, keepdims=True) * (1.0 / SAMPLES)
        for i in range(12):
            d = rec[pair, 128 * i : 128 * i + 128, :] - mean
            rec[pair, 128 * i : 128 * i + 128, :] = d
            hi, lo = split(jnp.abs(d))
            mag[HALF + 128 * i : HALF + 128 * i + 128, 0:128] = hi
            mag[HALF + 128 * i : HALF + 128 * i + 128, 128:256] = lo
        for i in range(12):
            both = jnp.dot(band, mag[128 * i : 128 * i + 256, :], preferred_element_type=jnp.float32)
            t = lax.broadcasted_iota(jnp.int32, (128, 128), 0) + 128 * i
            count = (jnp.minimum(t, HALF) + jnp.minimum(SAMPLES - 1 - t, HALF) + 1).astype(jnp.float32)
            running = (both[:, 0:128] + both[:, 128:256]) / count
            rec[pair, 128 * i : 128 * i + 128, :] = rec[pair, 128 * i : 128 * i + 128, :] / (running + epsilon)


def place(me, d, high, z):
    return pl.multiple_of(((high * 8 + z) * 4) * TAU + lax.rem(me[0] + 4 - d, 4) * TAU, 8)


def clear(seq):
    seq[0:64, :] = jnp.zeros((64, 128), jnp.float32)
    at = QFRONT + SAMPLES - 16
    seq[at : at + 80, :] = jnp.zeros((80, 128), jnp.float32)
    at = QFRONT + ROW + SAMPLES - 16
    seq[at:SEQ, :] = jnp.zeros((SEQ - at, 128), jnp.float32)


def moves(from_, to, sems, pair, start):
    copy = pltpu.make_async_copy(from_.at[pair], to.at[pair], sems.at[pair])
    if start:
        copy.start()
    else:
        copy.wait()


def p_side(me, p0, p1, p2, p3, out, rec, mag, seq, turned, lhs, sems):
    for d, ref in enumerate((p0, p1, p2, p3)):
        for high in range(2):
            for z in range(8):
                for pair in range(2):
                    rec[pair, pl.ds(place(me, d, high, z), TAU), :] = ref[z, pair, high]
    normalize(rec, mag)
    for pair in range(2):
        clear(seq)
        for i in range(12):
            x = rec[pair, 128 * i : 128 * i + 128, :]
            r = pltpu.roll(x, 64, 1)
            at = FRONT + 128 * i
            seq[at : at + 128, 0:64] = x[:, 0:64]
            seq[at - 16 : at + 112, 64:128] = r[:, 64:128]
            at += ROW
            seq[at : at + 128, 0:64] = r[:, 0:64]
            seq[at - 16 : at + 112, 64:128] = x[:, 64:128]
        for i in range(SEQ // 128):
            turned[:, 128 * i : 128 * i + 128] = seq[128 * i : 128 * i + 128, :].T
        for at in range(0, K, WIDE):
            for m in range(8):
                wide = turned[16 * m : 16 * m + 16, at : at + WIDE + 128]
                for r, rot in enumerate(ROT):
                    hi, lo = split(pltpu.roll(wide, WIDE + 128 - rot, 1)[:, 0:WIDE])
                    lhs[pair, 0, 128 * r + 16 * m : 128 * r + 16 * m + 16, at : at + WIDE] = hi
                    lhs[pair, 1, 128 * r + 16 * m : 128 * r + 16 * m + 16, at : at + WIDE] = lo
        moves(lhs, out, sems, pair, True)
    for pair in range(2):
        moves(lhs, out, sems, pair, False)


def correlate(me, q_in, p_in, keep, send, rec, mag, seq, lhs, rhs_hi, rhs_lo, acc, sems):
    for pair in range(2):
        moves(p_in, lhs, sems, pair, True)
    for d in range(4):
        for high in range(2):
            for z in range(8):
                for pair in range(2):
                    rec[pair, pl.ds(place(me, d, high, z), TAU), :] = q_in[z, d, pair, high]
    normalize(rec, mag)
    for pair in range(2):
        clear(seq.at[pair])
        for i in range(12):
            x = rec[pair, 128 * i : 128 * i + 128, :]
            r32, r64, r96 = (pltpu.roll(x, n, 1) for n in (32, 64, 96))
            at = QFRONT + 128 * i
            for e, parts in enumerate(((x, r32, r32, r64), (r64, r96, r96, x))):
                for n, part in enumerate(parts):
                    to = at + e * ROW - 8 * (n % 2)
                    seq[pair, to : to + 128, 32 * n : 32 * n + 32] = part[:, 32 * n : 32 * n + 32]
        moves(p_in, lhs, sems, pair, False)
        start = 0
        for n, width in enumerate(CHUNKS):
            for s in range(4):
                for m in range(width // 128):
                    at = start + 128 * m
                    hi, lo = split(seq[pair, at + s : at + s + 128, :])
                    rhs_hi[pair, at : at + 128, 128 * s : 128 * s + 128] = hi
                    rhs_lo[pair, at : at + 128, 128 * s : 128 * s + 128] = lo
            span = slice(start, start + width)
            part = jnp.dot(lhs[pair, 0, :, span], rhs_hi[pair, span, :], preferred_element_type=jnp.float32)
            part += jnp.dot(lhs[pair, 0, :, span], rhs_lo[pair, span, :], preferred_element_type=jnp.float32)
            part += jnp.dot(lhs[pair, 1, :, span], rhs_hi[pair, span, :], preferred_element_type=jnp.float32)
            if n or pair:
                acc[...] += part
            else:
                acc[...] = part
            start += width
    low = lanes((16, 128)) < 64
    first = me[1] == 0
    for g in range(8):
        for x in range(4):
            at = 64 * g + 16 * x
            for s2 in range(2):
                a = acc[at : at + 16, 256 * s2 : 256 * s2 + 128]
                b = acc[at : at + 16, 256 * s2 + 128 : 256 * s2 + 256]
                one = jnp.where(low, a, pltpu.roll(b, 64, 1))
                two = jnp.where(low, pltpu.roll(a, 64, 1), b)
                keep[x, g, s2] = jnp.where(first, one, two)
                send[x, g, s2] = jnp.where(first, two, one)


def final_kernel(got, out):
    lane = lanes((16, 128))
    for g in range(8):
        r, j = g // 2, g % 2
        r0, r1 = r % 2, r // 2
        for s2 in range(2):
            parts = [got[x, g, s2] for x in range(4)]
            for sb in range(2):
                for i in range(2):
                    mu = 2 * s2 + sb + 4 * (1 - r0) + 8 * i + 16 * (1 - j) + 32 * (1 - r1)
                    if mu == 0:
                        continue
                    n = 2 * sb + i
                    moved = [pltpu.roll(parts[x], (32 * (x - n)) % 128, 1) if x != n else parts[x] for x in range(4)]
                    value = jnp.where(lane < 32, moved[0], jnp.where(lane < 64, moved[1], jnp.where(lane < 96, moved[2], moved[3])))
                    out[mu - 1] = value * (1.0 / SAMPLES)


def sds(*shape, dtype=jnp.float32):
    return jax.ShapeDtypeStruct(shape, dtype)


def around(v, d):
    return lax.ppermute(v, "x", [(i, (i + d) % 4) for i in range(4)])


def copies(v):
    return jnp.broadcast_to(v[None], (8,) + v.shape)


def to_all(v):
    return lax.all_to_all(v, "z", 0, 0, tiled=True)


def local(raw):
    x = lax.axis_index("x")
    me = jnp.stack([x, lax.axis_index("core")]).astype(jnp.int32)
    sent = pl.pallas_call(prepack, out_shape=sds(8, TAU, 768), in_specs=[VMEM], out_specs=VMEM, compiler_params=SMALL, name="prepack")(raw[0])
    got = lax.all_to_all(sent, ("yh", "yl"), 0, 0, tiled=True)
    p_send, rest = pl.pallas_call(
        repack_p,
        out_shape=(sds(8, 2, 2, TAU, 128), sds(8, TAU, 256)),
        in_specs=[VMEM],
        out_specs=(VMEM, VMEM),
        compiler_params=SMALL,
        name="repack_p",
    )(got)
    p_mine = to_all(p_send)
    q_send = pl.pallas_call(
        repack_q,
        out_shape=sds(4, 2, 2, TAU, 128),
        in_specs=[SMEM, VMEM],
        out_specs=VMEM,
        compiler_params=SMALL,
        cost_estimate=pl.CostEstimate(flops=0, bytes_accessed=6 * 10**7, transcendentals=0),
        name="repack_q",
    )(me, rest)
    q_mine = [q_send[0]] + [around(q_send[d], d) for d in (1, 2, 3)]
    p_mine, *q_mine = lax.optimization_barrier((p_mine, *q_mine))
    q_all = to_all(copies(jnp.stack(q_mine)))
    p_all = [p_mine] + [around(p_mine, d) for d in (1, 2, 3)]
    shifted = pl.pallas_call(
        p_side,
        out_shape=sds(2, 2, 512, K, dtype=jnp.bfloat16),
        in_specs=[SMEM] + [VMEM] * 4,
        out_specs=HBM,
        scratch_shapes=[
            pltpu.VMEM((2, SAMPLES, 128), jnp.float32),
            pltpu.VMEM((SAMPLES + 2 * HALF, 256), jnp.bfloat16),
            pltpu.VMEM((SEQ, 128), jnp.float32),
            pltpu.VMEM((128, SEQ), jnp.float32),
            pltpu.VMEM((2, 2, 512, K), jnp.bfloat16),
            pltpu.SemaphoreType.DMA((2,)),
        ],
        compiler_params=pltpu.CompilerParams(vmem_limit_bytes=P_VMEM),
        cost_estimate=pl.CostEstimate(flops=10**9, bytes_accessed=20 * 10**6, transcendentals=0),
        name="p_side",
    )(me, *p_all)
    keep, send = pl.pallas_call(
        correlate,
        out_shape=(sds(4, 8, 2, 16, 128),) * 2,
        in_specs=[SMEM, VMEM, HBM],
        out_specs=(VMEM, VMEM),
        scratch_shapes=[
            pltpu.VMEM((2, SAMPLES, 128), jnp.float32),
            pltpu.VMEM((SAMPLES + 2 * HALF, 256), jnp.bfloat16),
            pltpu.VMEM((2, SEQ, 128), jnp.float32),
            pltpu.VMEM((2, 2, 512, K), jnp.bfloat16),
            pltpu.VMEM((2, K, 512), jnp.bfloat16),
            pltpu.VMEM((2, K, 512), jnp.bfloat16),
            pltpu.VMEM((512, 512), jnp.float32),
            pltpu.SemaphoreType.DMA((2,)),
        ],
        compiler_params=pltpu.CompilerParams(vmem_limit_bytes=Q_VMEM),
        cost_estimate=pl.CostEstimate(flops=10**10, bytes_accessed=20 * 10**6, transcendentals=0),
        name="correlate",
    )(me, q_all, shifted)
    summed = keep + lax.ppermute(send, "core", [(0, 1), (1, 0)])
    mine = lax.all_to_all(summed, "x", 0, 0, tiled=True)
    out = pl.pallas_call(final_kernel, out_shape=sds(LAGS, 16, 128), in_specs=[VMEM], out_specs=VMEM, compiler_params=SMALL, name="finish")(mine)
    return jnp.transpose(out, (1, 0, 2))


def solution(mesh):
    grid = Mesh(mesh.devices.reshape(2, 8, 4, 4, 2), ("yh", "z", "x", "yl", "core"))
    in_specs = (P(("yl", "core"), ("yh", "z", "x"), None),)
    out_specs = P(("yh", "z", "x"), None, ("yl", "core"))
    return jax.shard_map(local, mesh=grid, in_specs=in_specs, out_specs=out_specs, check_vma=False)
```

```python
import jax
import jax.numpy as jnp
from jax import lax
from jax.experimental import pallas as pl
from jax.experimental.pallas import tpu as pltpu
from jax.sharding import Mesh, PartitionSpec as P

C = 1024
MAXLAG = 31
HALF = 64
LAGS = 63
SAMPLES = 1536
epsilon = 1e-06

TAU = 24
ROW = SAMPLES + 32
K = 3328
FRONT = 40
QFRONT = FRONT - 24
SEQ = K + 128
CHUNKS = (768, 768, 768, 1024)
ROT = (4, 8, 36, 40)
VMEM = pl.BlockSpec(memory_space=pltpu.VMEM)
HBM = pl.BlockSpec(memory_space=pltpu.HBM)
SMEM = pl.BlockSpec(memory_space=pltpu.SMEM)
P_VMEM = 49 * 1024 * 1024
Q_VMEM = 49 * 1024 * 1024
SMALL = pltpu.CompilerParams(vmem_limit_bytes=8 * 1024 * 1024)


def lanes(shape):
    return lax.broadcasted_iota(jnp.int32, shape, len(shape) - 1)


def prepack(raw, out):
    lane = lanes((TAU, 128))
    for low in range(4):
        a = raw[:, 256 * low : 256 * low + 128]
        b = raw[:, 256 * low + 128 : 256 * low + 256]
        first = jnp.where(
            lane < 32, a, jnp.where(lane < 64, pltpu.roll(b, 32, 1), jnp.where(lane < 96, pltpu.roll(a, 32, 1), pltpu.roll(b, 64, 1)))
        )
        second = jnp.where(
            lane < 32, pltpu.roll(a, 64, 1), jnp.where(lane < 64, pltpu.roll(b, 96, 1), jnp.where(lane < 96, pltpu.roll(a, 96, 1), b))
        )
        for high in range(2):
            out[4 * high + low, :, 512:640] = first
            out[4 * high + low, :, 640:768] = second
            out[4 * high + low, :, 0:512] = raw[:, 512 * high : 512 * high + 512]


def pairs(got, high, pair, at):
    low = lanes((TAU, 128)) < 64
    a = got[4 * high + 2 * pair, :, at : at + 128]
    b = got[4 * high + 2 * pair + 1, :, at : at + 128]
    return jnp.where(low, a, pltpu.roll(b, 64, 1)), jnp.where(low, pltpu.roll(a, 64, 1), b)


def repack_p(got, out, rest):
    for high in range(2):
        for pair in range(2):
            for v in range(4):
                out[2 * v, pair, high], out[2 * v + 1, pair, high] = pairs(got, high, pair, 128 * v)
    rest[...] = got[:, :, 512:768]


def repack_q(me, got, out):
    for high in range(2):
        for pair in range(2):
            for v in range(2):
                for n, block in enumerate(pairs(got, high, pair, 128 * v)):
                    out[lax.rem(2 * v + n + 4 - me[0], 4), pair, high] = block


def split(x):
    hi = x.astype(jnp.bfloat16)
    return hi, (x - hi.astype(jnp.float32)).astype(jnp.bfloat16)


def normalize(rec, mag):
    row = lax.broadcasted_iota(jnp.int32, (128, 256), 0)
    col = lanes((128, 256))
    band = jnp.where((col >= row) & (col <= row + 2 * HALF), 1.0, 0.0).astype(jnp.bfloat16)
    zero = jnp.zeros((HALF, 256), jnp.bfloat16)
    mag[0:HALF, :] = zero
    mag[HALF + SAMPLES : 2 * HALF + SAMPLES, :] = zero
    for pair in range(2):
        mean = jnp.sum(rec[pair], axis=0, keepdims=True) * (1.0 / SAMPLES)
        for i in range(12):
            d = rec[pair, 128 * i : 128 * i + 128, :] - mean
            rec[pair, 128 * i : 128 * i + 128, :] = d
            hi, lo = split(jnp.abs(d))
            mag[HALF + 128 * i : HALF + 128 * i + 128, 0:128] = hi
            mag[HALF + 128 * i : HALF + 128 * i + 128, 128:256] = lo
        for i in range(12):
            both = jnp.dot(band, mag[128 * i : 128 * i + 256, :], preferred_element_type=jnp.float32)
            t = lax.broadcasted_iota(jnp.int32, (128, 128), 0) + 128 * i
            count = (jnp.minimum(t, HALF) + jnp.minimum(SAMPLES - 1 - t, HALF) + 1).astype(jnp.float32)
            running = (both[:, 0:128] + both[:, 128:256]) / count
            rec[pair, 128 * i : 128 * i + 128, :] = rec[pair, 128 * i : 128 * i + 128, :] / (running + epsilon)


def place(me, d, high, z):
    return pl.multiple_of(((high * 8 + z) * 4) * TAU + lax.rem(me[0] + 4 - d, 4) * TAU, 8)


def clear(seq):
    seq[0:64, :] = jnp.zeros((64, 128), jnp.float32)
    at = QFRONT + SAMPLES - 16
    seq[at : at + 80, :] = jnp.zeros((80, 128), jnp.float32)
    at = QFRONT + ROW + SAMPLES - 16
    seq[at:SEQ, :] = jnp.zeros((SEQ - at, 128), jnp.float32)


def moves(from_, to, sems, pair, start):
    copy = pltpu.make_async_copy(from_, to, sems.at[pair])
    if start:
        copy.start()
    else:
        copy.wait()


def p_side(me, p0, p1, p2, p3, out, rec, mag, seq, turned, sems):
    for d, ref in enumerate((p0, p1, p2, p3)):
        for high in range(2):
            for z in range(8):
                for pair in range(2):
                    rec[pair, pl.ds(place(me, d, high, z), TAU), :] = ref[z, pair, high]
    normalize(rec, mag)
    for pair in range(2):
        clear(seq.at[pair])
        for i in range(12):
            x = rec[pair, 128 * i : 128 * i + 128, :]
            r = pltpu.roll(x, 64, 1)
            at = FRONT + 128 * i
            seq[pair, at : at + 128, 0:64] = x[:, 0:64]
            seq[pair, at - 16 : at + 112, 64:128] = r[:, 64:128]
            at += ROW
            seq[pair, at : at + 128, 0:64] = r[:, 0:64]
            seq[pair, at - 16 : at + 112, 64:128] = x[:, 64:128]
        for i in range(SEQ // 128):
            turned[pair, :, 128 * i : 128 * i + 128] = seq[pair, 128 * i : 128 * i + 128, :].T
        moves(turned.at[pair], out.at[pair, 0], sems, pair, True)
    for pair in range(2):
        moves(turned.at[pair], out.at[pair, 0], sems, pair, False)


def correlate(me, q_in, p_in, keep, send, rec, mag, seq, turned, lhs_hi, lhs_lo, rhs_hi, rhs_lo, acc, sems):
    for pair in range(2):
        moves(p_in.at[pair, 0], turned.at[pair], sems, pair, True)
    for d in range(4):
        for high in range(2):
            for z in range(8):
                for pair in range(2):
                    rec[pair, pl.ds(place(me, d, high, z), TAU), :] = q_in[z, d, pair, high]
    normalize(rec, mag)
    for pair in range(2):
        clear(seq.at[pair])
        for i in range(12):
            x = rec[pair, 128 * i : 128 * i + 128, :]
            r32, r64, r96 = (pltpu.roll(x, n, 1) for n in (32, 64, 96))
            at = QFRONT + 128 * i
            for e, parts in enumerate(((x, r32, r32, r64), (r64, r96, r96, x))):
                for n, part in enumerate(parts):
                    to = at + e * ROW - 8 * (n % 2)
                    seq[pair, to : to + 128, 32 * n : 32 * n + 32] = part[:, 32 * n : 32 * n + 32]
        moves(p_in.at[pair, 0], turned.at[pair], sems, pair, False)
        start = 0
        for n, width in enumerate(CHUNKS):
            for m in range(8):
                wide = turned[pair, 16 * m : 16 * m + 16, start : start + width + 128]
                for r, rot in enumerate(ROT):
                    hi, lo = split(pltpu.roll(wide, width + 128 - rot, 1)[:, 0:width])
                    lhs_hi[pair, 128 * r + 16 * m : 128 * r + 16 * m + 16, start : start + width] = hi
                    lhs_lo[pair, 128 * r + 16 * m : 128 * r + 16 * m + 16, start : start + width] = lo
            for s in range(4):
                for m in range(width // 128):
                    at = start + 128 * m
                    hi, lo = split(seq[pair, at + s : at + s + 128, :])
                    rhs_hi[pair, at : at + 128, 128 * s : 128 * s + 128] = hi
                    rhs_lo[pair, at : at + 128, 128 * s : 128 * s + 128] = lo
            span = slice(start, start + width)
            part = jnp.dot(lhs_hi[pair, :, span], rhs_hi[pair, span, :], preferred_element_type=jnp.float32)
            part += jnp.dot(lhs_hi[pair, :, span], rhs_lo[pair, span, :], preferred_element_type=jnp.float32)
            part += jnp.dot(lhs_lo[pair, :, span], rhs_hi[pair, span, :], preferred_element_type=jnp.float32)
            if n or pair:
                acc[...] += part
            else:
                acc[...] = part
            start += width
    low = lanes((16, 128)) < 64
    first = me[1] == 0
    for g in range(8):
        for x in range(4):
            at = 64 * g + 16 * x
            for s2 in range(2):
                a = acc[at : at + 16, 256 * s2 : 256 * s2 + 128]
                b = acc[at : at + 16, 256 * s2 + 128 : 256 * s2 + 256]
                one = jnp.where(low, a, pltpu.roll(b, 64, 1))
                two = jnp.where(low, pltpu.roll(a, 64, 1), b)
                keep[x, g, s2] = jnp.where(first, one, two)
                send[x, g, s2] = jnp.where(first, two, one)


def final_kernel(got, out):
    lane = lanes((16, 128))
    for g in range(8):
        r, j = g // 2, g % 2
        r0, r1 = r % 2, r // 2
        for s2 in range(2):
            parts = [got[x, g, s2] for x in range(4)]
            for sb in range(2):
                for i in range(2):
                    mu = 2 * s2 + sb + 4 * (1 - r0) + 8 * i + 16 * (1 - j) + 32 * (1 - r1)
                    if mu == 0:
                        continue
                    n = 2 * sb + i
                    moved = [pltpu.roll(parts[x], (32 * (x - n)) % 128, 1) if x != n else parts[x] for x in range(4)]
                    value = jnp.where(lane < 32, moved[0], jnp.where(lane < 64, moved[1], jnp.where(lane < 96, moved[2], moved[3])))
                    out[mu - 1] = value * (1.0 / SAMPLES)


def sds(*shape, dtype=jnp.float32):
    return jax.ShapeDtypeStruct(shape, dtype)


def around(v, d):
    return lax.ppermute(v, "x", [(i, (i + d) % 4) for i in range(4)])


def copies(v):
    return jnp.broadcast_to(v[None], (8,) + v.shape)


def to_all(v):
    return lax.all_to_all(v, "z", 0, 0, tiled=True)


def local(raw):
    x = lax.axis_index("x")
    me = jnp.stack([x, lax.axis_index("core")]).astype(jnp.int32)
    sent = pl.pallas_call(prepack, out_shape=sds(8, TAU, 768), in_specs=[VMEM], out_specs=VMEM, compiler_params=SMALL, name="prepack")(raw[0])
    got = lax.all_to_all(sent, ("yh", "yl"), 0, 0, tiled=True)
    p_send, rest = pl.pallas_call(
        repack_p,
        out_shape=(sds(8, 2, 2, TAU, 128), sds(8, TAU, 256)),
        in_specs=[VMEM],
        out_specs=(VMEM, VMEM),
        compiler_params=SMALL,
        name="repack_p",
    )(got)
    p_mine = to_all(p_send)
    q_send = pl.pallas_call(
        repack_q,
        out_shape=sds(4, 2, 2, TAU, 128),
        in_specs=[SMEM, VMEM],
        out_specs=VMEM,
        compiler_params=SMALL,
        cost_estimate=pl.CostEstimate(flops=0, bytes_accessed=6 * 10**7, transcendentals=0),
        name="repack_q",
    )(me, rest)
    q_mine = [q_send[0]] + [around(q_send[d], d) for d in (1, 2, 3)]
    p_mine, *q_mine = lax.optimization_barrier((p_mine, *q_mine))
    q_all = to_all(copies(jnp.stack(q_mine)))
    p_all = [p_mine] + [around(p_mine, d) for d in (1, 2, 3)]
    p_done = pl.pallas_call(
        p_side,
        out_shape=sds(2, 4, 128, SEQ),
        in_specs=[SMEM] + [VMEM] * 4,
        out_specs=HBM,
        scratch_shapes=[
            pltpu.VMEM((2, SAMPLES, 128), jnp.float32),
            pltpu.VMEM((SAMPLES + 2 * HALF, 256), jnp.bfloat16),
            pltpu.VMEM((2, SEQ, 128), jnp.float32),
            pltpu.VMEM((2, 128, SEQ), jnp.float32),
            pltpu.SemaphoreType.DMA((2,)),
        ],
        compiler_params=pltpu.CompilerParams(vmem_limit_bytes=P_VMEM),
        cost_estimate=pl.CostEstimate(flops=10**9, bytes_accessed=20 * 10**6, transcendentals=0),
        name="p_side",
    )(me, *p_all)
    keep, send = pl.pallas_call(
        correlate,
        out_shape=(sds(4, 8, 2, 16, 128),) * 2,
        in_specs=[SMEM, VMEM, HBM],
        out_specs=(VMEM, VMEM),
        scratch_shapes=[
            pltpu.VMEM((2, SAMPLES, 128), jnp.float32),
            pltpu.VMEM((SAMPLES + 2 * HALF, 256), jnp.bfloat16),
            pltpu.VMEM((2, SEQ, 128), jnp.float32),
            pltpu.VMEM((2, 128, SEQ), jnp.float32),
            pltpu.VMEM((2, 512, K), jnp.bfloat16),
            pltpu.VMEM((2, 512, K), jnp.bfloat16),
            pltpu.VMEM((2, K, 512), jnp.bfloat16),
            pltpu.VMEM((2, K, 512), jnp.bfloat16),
            pltpu.VMEM((512, 512), jnp.float32),
            pltpu.SemaphoreType.DMA((2,)),
        ],
        compiler_params=pltpu.CompilerParams(vmem_limit_bytes=Q_VMEM),
        cost_estimate=pl.CostEstimate(flops=10**10, bytes_accessed=20 * 10**6, transcendentals=0),
        name="correlate",
    )(me, q_all, p_done)
    summed = keep + lax.ppermute(send, "core", [(0, 1), (1, 0)])
    mine = lax.all_to_all(summed, "x", 0, 0, tiled=True)
    out = pl.pallas_call(final_kernel, out_shape=sds(LAGS, 16, 128), in_specs=[VMEM], out_specs=VMEM, compiler_params=SMALL, name="finish")(mine)
    return jnp.transpose(out, (1, 0, 2))


def solution(mesh):
    grid = Mesh(mesh.devices.reshape(2, 8, 4, 4, 2), ("yh", "z", "x", "yl", "core"))
    in_specs = (P(("yl", "core"), ("yh", "z", "x"), None),)
    out_specs = P(("yh", "z", "x"), None, ("yl", "core"))
    return jax.shard_map(local, mesh=grid, in_specs=in_specs, out_specs=out_specs, check_vma=False)
```

```python
import jax
import jax.numpy as jnp
from jax import lax
from jax.experimental import pallas as pl
from jax.experimental.pallas import tpu as pltpu
from jax.sharding import Mesh, PartitionSpec as P

C = 1024
MAXLAG = 31
HALF = 64
LAGS = 63
SAMPLES = 1536
epsilon = 1e-06

TAU = 24
ROW = SAMPLES + 32
K = 3200
FRONT = 40
QFRONT = FRONT - 24
SEQ = K + 128
CHUNKS = (1024, 1024, 1152)
ROT = (4, 8, 36, 40)
VMEM = pl.BlockSpec(memory_space=pltpu.VMEM)
HBM = pl.BlockSpec(memory_space=pltpu.HBM)
SMEM = pl.BlockSpec(memory_space=pltpu.SMEM)
P_VMEM = 49 * 1024 * 1024
Q_VMEM = 49 * 1024 * 1024
SMALL = pltpu.CompilerParams(vmem_limit_bytes=8 * 1024 * 1024)


def lanes(shape):
    return lax.broadcasted_iota(jnp.int32, shape, len(shape) - 1)


def prepack(raw, out):
    lane = lanes((TAU, 128))
    for low in range(4):
        a = raw[:, 256 * low : 256 * low + 128]
        b = raw[:, 256 * low + 128 : 256 * low + 256]
        first = jnp.where(
            lane < 32, a, jnp.where(lane < 64, pltpu.roll(b, 32, 1), jnp.where(lane < 96, pltpu.roll(a, 32, 1), pltpu.roll(b, 64, 1)))
        )
        second = jnp.where(
            lane < 32, pltpu.roll(a, 64, 1), jnp.where(lane < 64, pltpu.roll(b, 96, 1), jnp.where(lane < 96, pltpu.roll(a, 96, 1), b))
        )
        for high in range(2):
            out[4 * high + low, :, 512:640] = first
            out[4 * high + low, :, 640:768] = second
            out[4 * high + low, :, 0:512] = raw[:, 512 * high : 512 * high + 512]


def pairs(got, high, pair, at):
    low = lanes((TAU, 128)) < 64
    a = got[4 * high + 2 * pair, :, at : at + 128]
    b = got[4 * high + 2 * pair + 1, :, at : at + 128]
    return jnp.where(low, a, pltpu.roll(b, 64, 1)), jnp.where(low, pltpu.roll(a, 64, 1), b)


def repack(me, got, p_out, q_out):
    for high in range(2):
        for pair in range(2):
            for v in range(4):
                p_out[2 * v, pair, high], p_out[2 * v + 1, pair, high] = pairs(got, high, pair, 128 * v)
            for v in range(2):
                for n, block in enumerate(pairs(got, high, pair, 512 + 128 * v)):
                    q_out[lax.rem(2 * v + n + 4 - me[0], 4), pair, high] = block


def split(x):
    hi = x.astype(jnp.bfloat16)
    return hi, (x - hi.astype(jnp.float32)).astype(jnp.bfloat16)


def normalize(rec, mag):
    row = lax.broadcasted_iota(jnp.int32, (128, 256), 0)
    col = lanes((128, 256))
    band = jnp.where((col >= row) & (col <= row + 2 * HALF), 1.0, 0.0).astype(jnp.bfloat16)
    zero = jnp.zeros((HALF, 256), jnp.bfloat16)
    mag[0:HALF, :] = zero
    mag[HALF + SAMPLES : 2 * HALF + SAMPLES, :] = zero
    for pair in range(2):
        mean = jnp.sum(rec[pair], axis=0, keepdims=True) * (1.0 / SAMPLES)
        for i in range(12):
            d = rec[pair, 128 * i : 128 * i + 128, :] - mean
            rec[pair, 128 * i : 128 * i + 128, :] = d
            hi, lo = split(jnp.abs(d))
            mag[HALF + 128 * i : HALF + 128 * i + 128, 0:128] = hi
            mag[HALF + 128 * i : HALF + 128 * i + 128, 128:256] = lo
        for i in range(12):
            both = jnp.dot(band, mag[128 * i : 128 * i + 256, :], preferred_element_type=jnp.float32)
            t = lax.broadcasted_iota(jnp.int32, (128, 128), 0) + 128 * i
            count = (jnp.minimum(t, HALF) + jnp.minimum(SAMPLES - 1 - t, HALF) + 1).astype(jnp.float32)
            running = (both[:, 0:128] + both[:, 128:256]) / count
            rec[pair, 128 * i : 128 * i + 128, :] = rec[pair, 128 * i : 128 * i + 128, :] / (running + epsilon)


def place(me, d, high, z):
    return pl.multiple_of(((high * 8 + z) * 4) * TAU + lax.rem(me[0] + 4 - d, 4) * TAU, 8)


def clear(seq):
    seq[0:64, :] = jnp.zeros((64, 128), jnp.float32)
    at = QFRONT + SAMPLES - 16
    seq[at : at + 80, :] = jnp.zeros((80, 128), jnp.float32)
    at = QFRONT + ROW + SAMPLES - 16
    seq[at:SEQ, :] = jnp.zeros((SEQ - at, 128), jnp.float32)


def moves(from_, to, sems, pair, start):
    copy = pltpu.make_async_copy(from_, to, sems.at[pair])
    if start:
        copy.start()
    else:
        copy.wait()


def p_side(me, p0, p1, p2, p3, out, rec, mag, seq, turned, sems):
    for d, ref in enumerate((p0, p1, p2, p3)):
        for high in range(2):
            for z in range(8):
                for pair in range(2):
                    rec[pair, pl.ds(place(me, d, high, z), TAU), :] = ref[z, pair, high]
    normalize(rec, mag)
    for pair in range(2):
        clear(seq.at[pair])
        for i in range(12):
            x = rec[pair, 128 * i : 128 * i + 128, :]
            r = pltpu.roll(x, 64, 1)
            at = FRONT + 128 * i
            seq[pair, at : at + 128, 0:64] = x[:, 0:64]
            seq[pair, at - 16 : at + 112, 64:128] = r[:, 64:128]
            at += ROW
            seq[pair, at : at + 128, 0:64] = r[:, 0:64]
            seq[pair, at - 16 : at + 112, 64:128] = x[:, 64:128]
        for i in range(SEQ // 128):
            turned[pair, :, 128 * i : 128 * i + 128] = seq[pair, 128 * i : 128 * i + 128, :].T
        moves(turned.at[pair], out.at[pair, 0], sems, pair, True)
    for pair in range(2):
        moves(turned.at[pair], out.at[pair, 0], sems, pair, False)


def correlate(me, q_in, p_in, keep, send, rec, mag, seq, turned, lhs_hi, lhs_lo, rhs_hi, rhs_lo, acc, sems):
    for pair in range(2):
        moves(p_in.at[pair, 0], turned.at[pair], sems, pair, True)
    for d in range(4):
        for high in range(2):
            for z in range(8):
                for pair in range(2):
                    rec[pair, pl.ds(place(me, d, high, z), TAU), :] = q_in[z, d, pair, high]
    normalize(rec, mag)
    for pair in range(2):
        clear(seq.at[pair])
        for i in range(12):
            x = rec[pair, 128 * i : 128 * i + 128, :]
            r32, r64, r96 = (pltpu.roll(x, n, 1) for n in (32, 64, 96))
            at = QFRONT + 128 * i
            for e, parts in enumerate(((x, r32, r32, r64), (r64, r96, r96, x))):
                for n, part in enumerate(parts):
                    to = at + e * ROW - 8 * (n % 2)
                    seq[pair, to : to + 128, 32 * n : 32 * n + 32] = part[:, 32 * n : 32 * n + 32]
        moves(p_in.at[pair, 0], turned.at[pair], sems, pair, False)
        start = 0
        for n, width in enumerate(CHUNKS):
            for m in range(8):
                wide = turned[pair, 16 * m : 16 * m + 16, start : start + width + 128]
                for r, rot in enumerate(ROT):
                    hi, lo = split(pltpu.roll(wide, width + 128 - rot, 1)[:, 0:width])
                    lhs_hi[pair, 128 * r + 16 * m : 128 * r + 16 * m + 16, start : start + width] = hi
                    lhs_lo[pair, 128 * r + 16 * m : 128 * r + 16 * m + 16, start : start + width] = lo
            for s in range(4):
                for m in range(width // 128):
                    at = start + 128 * m
                    hi, lo = split(seq[pair, at + s : at + s + 128, :])
                    rhs_hi[pair, at : at + 128, 128 * s : 128 * s + 128] = hi
                    rhs_lo[pair, at : at + 128, 128 * s : 128 * s + 128] = lo
            span = slice(start, start + width)
            part = jnp.dot(lhs_hi[pair, :, span], rhs_hi[pair, span, :], preferred_element_type=jnp.float32)
            part += jnp.dot(lhs_hi[pair, :, span], rhs_lo[pair, span, :], preferred_element_type=jnp.float32)
            part += jnp.dot(lhs_lo[pair, :, span], rhs_hi[pair, span, :], preferred_element_type=jnp.float32)
            if n or pair:
                acc[...] += part
            else:
                acc[...] = part
            start += width
    low = lanes((16, 128)) < 64
    first = me[1] == 0
    for g in range(8):
        for x in range(4):
            at = 64 * g + 16 * x
            for s2 in range(2):
                a = acc[at : at + 16, 256 * s2 : 256 * s2 + 128]
                b = acc[at : at + 16, 256 * s2 + 128 : 256 * s2 + 256]
                one = jnp.where(low, a, pltpu.roll(b, 64, 1))
                two = jnp.where(low, pltpu.roll(a, 64, 1), b)
                keep[x, g, s2] = jnp.where(first, one, two)
                send[x, g, s2] = jnp.where(first, two, one)


def final_kernel(got, out):
    lane = lanes((16, 128))
    for g in range(8):
        r, j = g // 2, g % 2
        r0, r1 = r % 2, r // 2
        for s2 in range(2):
            parts = [got[x, g, s2] for x in range(4)]
            for sb in range(2):
                for i in range(2):
                    mu = 2 * s2 + sb + 4 * (1 - r0) + 8 * i + 16 * (1 - j) + 32 * (1 - r1)
                    if mu == 0:
                        continue
                    n = 2 * sb + i
                    moved = [pltpu.roll(parts[x], (32 * (x - n)) % 128, 1) if x != n else parts[x] for x in range(4)]
                    value = jnp.where(lane < 32, moved[0], jnp.where(lane < 64, moved[1], jnp.where(lane < 96, moved[2], moved[3])))
                    out[mu - 1] = value * (1.0 / SAMPLES)


def sds(*shape, dtype=jnp.float32):
    return jax.ShapeDtypeStruct(shape, dtype)


def around(v, d):
    return lax.ppermute(v, "x", [(i, (i + d) % 4) for i in range(4)])


def copies(v):
    return jnp.broadcast_to(v[None], (8,) + v.shape)


def to_all(v):
    return lax.all_to_all(v, "z", 0, 0, tiled=True)


def local(raw):
    x = lax.axis_index("x")
    me = jnp.stack([x, lax.axis_index("core")]).astype(jnp.int32)
    sent = pl.pallas_call(prepack, out_shape=sds(8, TAU, 768), in_specs=[VMEM], out_specs=VMEM, compiler_params=SMALL, name="prepack")(raw[0])
    got = lax.all_to_all(sent, ("yh", "yl"), 0, 0, tiled=True)
    p_send, q_send = pl.pallas_call(
        repack,
        out_shape=(sds(8, 2, 2, TAU, 128), sds(4, 2, 2, TAU, 128)),
        in_specs=[SMEM, VMEM],
        out_specs=(VMEM, VMEM),
        compiler_params=SMALL,
        name="repack",
    )(me, got)
    p_mine = to_all(p_send)
    q_mine = [q_send[0]] + [around(q_send[d], d) for d in (1, 2, 3)]
    p_mine, *q_mine = lax.optimization_barrier((p_mine, *q_mine))
    q_all = to_all(copies(jnp.stack(q_mine)))
    p_all = [p_mine] + [around(p_mine, d) for d in (1, 2, 3)]
    p_done = pl.pallas_call(
        p_side,
        out_shape=sds(2, 4, 128, SEQ),
        in_specs=[SMEM] + [VMEM] * 4,
        out_specs=HBM,
        scratch_shapes=[
            pltpu.VMEM((2, SAMPLES, 128), jnp.float32),
            pltpu.VMEM((SAMPLES + 2 * HALF, 256), jnp.bfloat16),
            pltpu.VMEM((2, SEQ, 128), jnp.float32),
            pltpu.VMEM((2, 128, SEQ), jnp.float32),
            pltpu.SemaphoreType.DMA((2,)),
        ],
        compiler_params=pltpu.CompilerParams(vmem_limit_bytes=P_VMEM),
        cost_estimate=pl.CostEstimate(flops=10**9, bytes_accessed=20 * 10**6, transcendentals=0),
        name="p_side",
    )(me, *p_all)
    keep, send = pl.pallas_call(
        correlate,
        out_shape=(sds(4, 8, 2, 16, 128),) * 2,
        in_specs=[SMEM, VMEM, HBM],
        out_specs=(VMEM, VMEM),
        scratch_shapes=[
            pltpu.VMEM((2, SAMPLES, 128), jnp.float32),
            pltpu.VMEM((SAMPLES + 2 * HALF, 256), jnp.bfloat16),
            pltpu.VMEM((2, SEQ, 128), jnp.float32),
            pltpu.VMEM((2, 128, SEQ), jnp.float32),
            pltpu.VMEM((2, 512, K), jnp.bfloat16),
            pltpu.VMEM((2, 512, K), jnp.bfloat16),
            pltpu.VMEM((2, K, 512), jnp.bfloat16),
            pltpu.VMEM((2, K, 512), jnp.bfloat16),
            pltpu.VMEM((512, 512), jnp.float32),
            pltpu.SemaphoreType.DMA((2,)),
        ],
        compiler_params=pltpu.CompilerParams(vmem_limit_bytes=Q_VMEM),
        cost_estimate=pl.CostEstimate(flops=10**10, bytes_accessed=20 * 10**6, transcendentals=0),
        name="correlate",
    )(me, q_all, p_done)
    summed = keep + lax.ppermute(send, "core", [(0, 1), (1, 0)])
    mine = lax.all_to_all(summed, "x", 0, 0, tiled=True)
    out = pl.pallas_call(final_kernel, out_shape=sds(LAGS, 16, 128), in_specs=[VMEM], out_specs=VMEM, compiler_params=SMALL, name="finish")(mine)
    return jnp.transpose(out, (1, 0, 2))


def solution(mesh):
    grid = Mesh(mesh.devices.reshape(2, 8, 4, 4, 2), ("yh", "z", "x", "yl", "core"))
    in_specs = (P(("yl", "core"), ("yh", "z", "x"), None),)
    out_specs = P(("yh", "z", "x"), None, ("yl", "core"))
    return jax.shard_map(local, mesh=grid, in_specs=in_specs, out_specs=out_specs, check_vma=False)
```

```python
import jax
import jax.numpy as jnp
from jax import lax
from jax.experimental import pallas as pl
from jax.experimental.pallas import tpu as pltpu
from jax.sharding import Mesh, PartitionSpec as P

C = 1024
MAXLAG = 31
HALF = 64
LAGS = 63
SAMPLES = 1536
epsilon = 1e-06

TAU = 24
ROW = SAMPLES + 32
K = 3328
FRONT = 40
QFRONT = FRONT - 24
SEQ = K + 128
CHUNKS = (768, 768, 768, 1024)
ROT = (4, 8, 36, 40)
VMEM = pl.BlockSpec(memory_space=pltpu.VMEM)
HBM = pl.BlockSpec(memory_space=pltpu.HBM)
SMEM = pl.BlockSpec(memory_space=pltpu.SMEM)
P_VMEM = 49 * 1024 * 1024
Q_VMEM = 49 * 1024 * 1024
SMALL = pltpu.CompilerParams(vmem_limit_bytes=8 * 1024 * 1024)


def lanes(shape):
    return lax.broadcasted_iota(jnp.int32, shape, len(shape) - 1)


def prepack(raw, out):
    lane = lanes((TAU, 128))
    for low in range(4):
        a = raw[:, 256 * low : 256 * low + 128]
        b = raw[:, 256 * low + 128 : 256 * low + 256]
        first = jnp.where(
            lane < 32, a, jnp.where(lane < 64, pltpu.roll(b, 32, 1), jnp.where(lane < 96, pltpu.roll(a, 32, 1), pltpu.roll(b, 64, 1)))
        )
        second = jnp.where(
            lane < 32, pltpu.roll(a, 64, 1), jnp.where(lane < 64, pltpu.roll(b, 96, 1), jnp.where(lane < 96, pltpu.roll(a, 96, 1), b))
        )
        for high in range(2):
            out[4 * high + low, :, 512:640] = first
            out[4 * high + low, :, 640:768] = second
            out[4 * high + low, :, 0:512] = raw[:, 512 * high : 512 * high + 512]


def pairs(got, high, pair, at):
    low = lanes((TAU, 128)) < 64
    a = got[4 * high + 2 * pair, :, at : at + 128]
    b = got[4 * high + 2 * pair + 1, :, at : at + 128]
    return jnp.where(low, a, pltpu.roll(b, 64, 1)), jnp.where(low, pltpu.roll(a, 64, 1), b)


def repack_p(got, out, rest):
    for high in range(2):
        for pair in range(2):
            for v in range(4):
                out[2 * v, pair, high], out[2 * v + 1, pair, high] = pairs(got, high, pair, 128 * v)
    rest[...] = got[:, :, 512:768]


def repack_q(me, got, out):
    for high in range(2):
        for pair in range(2):
            for v in range(2):
                for n, block in enumerate(pairs(got, high, pair, 128 * v)):
                    out[lax.rem(2 * v + n + 4 - me[0], 4), pair, high] = block


def split(x):
    hi = x.astype(jnp.bfloat16)
    return hi, (x - hi.astype(jnp.float32)).astype(jnp.bfloat16)


def normalize(rec, mag):
    row = lax.broadcasted_iota(jnp.int32, (128, 256), 0)
    col = lanes((128, 256))
    band = jnp.where((col >= row) & (col <= row + 2 * HALF), 1.0, 0.0).astype(jnp.bfloat16)
    zero = jnp.zeros((HALF, 256), jnp.bfloat16)
    mag[0:HALF, :] = zero
    mag[HALF + SAMPLES : 2 * HALF + SAMPLES, :] = zero
    for pair in range(2):
        mean = jnp.sum(rec[pair], axis=0, keepdims=True) * (1.0 / SAMPLES)
        for i in range(12):
            d = rec[pair, 128 * i : 128 * i + 128, :] - mean
            rec[pair, 128 * i : 128 * i + 128, :] = d
            hi, lo = split(jnp.abs(d))
            mag[HALF + 128 * i : HALF + 128 * i + 128, 0:128] = hi
            mag[HALF + 128 * i : HALF + 128 * i + 128, 128:256] = lo
        for i in range(12):
            both = jnp.dot(band, mag[128 * i : 128 * i + 256, :], preferred_element_type=jnp.float32)
            t = lax.broadcasted_iota(jnp.int32, (128, 128), 0) + 128 * i
            count = (jnp.minimum(t, HALF) + jnp.minimum(SAMPLES - 1 - t, HALF) + 1).astype(jnp.float32)
            running = (both[:, 0:128] + both[:, 128:256]) / count
            rec[pair, 128 * i : 128 * i + 128, :] = rec[pair, 128 * i : 128 * i + 128, :] / (running + epsilon)


def place(me, d, high, z):
    return pl.multiple_of(((high * 8 + z) * 4) * TAU + lax.rem(me[0] + 4 - d, 4) * TAU, 8)


def clear(seq):
    seq[0:64, :] = jnp.zeros((64, 128), jnp.float32)
    at = QFRONT + SAMPLES - 16
    seq[at : at + 80, :] = jnp.zeros((80, 128), jnp.float32)
    at = QFRONT + ROW + SAMPLES - 16
    seq[at:SEQ, :] = jnp.zeros((SEQ - at, 128), jnp.float32)


def moves(from_, to, sems, pair, start):
    copy = pltpu.make_async_copy(from_, to, sems.at[pair])
    if start:
        copy.start()
    else:
        copy.wait()


def p_side(me, p0, p1, p2, p3, out, rec, mag, seq, turned, sems):
    for d, ref in enumerate((p0, p1, p2, p3)):
        for high in range(2):
            for z in range(8):
                for pair in range(2):
                    rec[pair, pl.ds(place(me, d, high, z), TAU), :] = ref[z, pair, high]
    normalize(rec, mag)
    for pair in range(2):
        clear(seq.at[pair])
        for i in range(12):
            x = rec[pair, 128 * i : 128 * i + 128, :]
            r = pltpu.roll(x, 64, 1)
            at = FRONT + 128 * i
            seq[pair, at : at + 128, 0:64] = x[:, 0:64]
            seq[pair, at - 16 : at + 112, 64:128] = r[:, 64:128]
            at += ROW
            seq[pair, at : at + 128, 0:64] = r[:, 0:64]
            seq[pair, at - 16 : at + 112, 64:128] = x[:, 64:128]
        for i in range(SEQ // 128):
            turned[pair, :, 128 * i : 128 * i + 128] = seq[pair, 128 * i : 128 * i + 128, :].T
        moves(turned.at[pair], out.at[pair, 0], sems, pair, True)
    for pair in range(2):
        moves(turned.at[pair], out.at[pair, 0], sems, pair, False)


def correlate(me, q_in, p_in, keep, send, rec, mag, seq, turned, lhs_hi, lhs_lo, rhs_hi, rhs_lo, acc, sems):
    for pair in range(2):
        moves(p_in.at[pair, 0], turned.at[pair], sems, pair, True)
    for d in range(4):
        for high in range(2):
            for z in range(8):
                for pair in range(2):
                    rec[pair, pl.ds(place(me, d, high, z), TAU), :] = q_in[z, d, pair, high]
    normalize(rec, mag)
    for pair in range(2):
        clear(seq.at[pair])
        for i in range(12):
            x = rec[pair, 128 * i : 128 * i + 128, :]
            r32, r64, r96 = (pltpu.roll(x, n, 1) for n in (32, 64, 96))
            at = QFRONT + 128 * i
            for e, parts in enumerate(((x, r32, r32, r64), (r64, r96, r96, x))):
                for n, part in enumerate(parts):
                    to = at + e * ROW - 8 * (n % 2)
                    seq[pair, to : to + 128, 32 * n : 32 * n + 32] = part[:, 32 * n : 32 * n + 32]
        moves(p_in.at[pair, 0], turned.at[pair], sems, pair, False)
        start = 0
        for n, width in enumerate(CHUNKS):
            for m in range(8):
                wide = turned[pair, 16 * m : 16 * m + 16, start : start + width + 128]
                for r, rot in enumerate(ROT):
                    hi, lo = split(pltpu.roll(wide, width + 128 - rot, 1)[:, 0:width])
                    lhs_hi[pair, 128 * r + 16 * m : 128 * r + 16 * m + 16, start : start + width] = hi
                    lhs_lo[pair, 128 * r + 16 * m : 128 * r + 16 * m + 16, start : start + width] = lo
            for s in range(4):
                for m in range(width // 128):
                    at = start + 128 * m
                    hi, lo = split(seq[pair, at + s : at + s + 128, :])
                    rhs_hi[pair, at : at + 128, 128 * s : 128 * s + 128] = hi
                    rhs_lo[pair, at : at + 128, 128 * s : 128 * s + 128] = lo
            span = slice(start, start + width)
            part = jnp.dot(lhs_hi[pair, :, span], rhs_hi[pair, span, :], preferred_element_type=jnp.float32)
            part += jnp.dot(lhs_hi[pair, :, span], rhs_lo[pair, span, :], preferred_element_type=jnp.float32)
            part += jnp.dot(lhs_lo[pair, :, span], rhs_hi[pair, span, :], preferred_element_type=jnp.float32)
            if n or pair:
                acc[...] += part
            else:
                acc[...] = part
            start += width
    low = lanes((16, 128)) < 64
    first = me[1] == 0
    for g in range(8):
        for x in range(4):
            at = 64 * g + 16 * x
            ahead = lax.rem(x + 4 - me[0], 4)
            for s2 in range(2):
                a = acc[at : at + 16, 256 * s2 : 256 * s2 + 128]
                b = acc[at : at + 16, 256 * s2 + 128 : 256 * s2 + 256]
                one = jnp.where(low, a, pltpu.roll(b, 64, 1))
                two = jnp.where(low, pltpu.roll(a, 64, 1), b)
                keep[ahead, g, s2] = jnp.where(first, one, two)
                send[ahead, g, s2] = jnp.where(first, two, one)


def final_kernel(me, p0, p1, p2, p3, out, got):
    for d, ref in enumerate((p0, p1, p2, p3)):
        got[lax.rem(me[0] + 4 - d, 4)] = ref[...]
    lane = lanes((16, 128))
    for g in range(8):
        r, j = g // 2, g % 2
        r0, r1 = r % 2, r // 2
        for s2 in range(2):
            parts = [got[x, g, s2] for x in range(4)]
            for sb in range(2):
                for i in range(2):
                    mu = 2 * s2 + sb + 4 * (1 - r0) + 8 * i + 16 * (1 - j) + 32 * (1 - r1)
                    if mu == 0:
                        continue
                    n = 2 * sb + i
                    moved = [pltpu.roll(parts[x], (32 * (x - n)) % 128, 1) if x != n else parts[x] for x in range(4)]
                    value = jnp.where(lane < 32, moved[0], jnp.where(lane < 64, moved[1], jnp.where(lane < 96, moved[2], moved[3])))
                    out[mu - 1] = value * (1.0 / SAMPLES)


def sds(*shape, dtype=jnp.float32):
    return jax.ShapeDtypeStruct(shape, dtype)


def around(v, d):
    return lax.ppermute(v, "x", [(i, (i + d) % 4) for i in range(4)])


def copies(v):
    return jnp.broadcast_to(v[None], (8,) + v.shape)


def to_all(v):
    return lax.all_to_all(v, "z", 0, 0, tiled=True)


def local(raw):
    x = lax.axis_index("x")
    me = jnp.stack([x, lax.axis_index("core")]).astype(jnp.int32)
    sent = pl.pallas_call(prepack, out_shape=sds(8, TAU, 768), in_specs=[VMEM], out_specs=VMEM, compiler_params=SMALL, name="prepack")(raw[0])
    got = lax.all_to_all(sent, ("yh", "yl"), 0, 0, tiled=True)
    p_send, rest = pl.pallas_call(
        repack_p,
        out_shape=(sds(8, 2, 2, TAU, 128), sds(8, TAU, 256)),
        in_specs=[VMEM],
        out_specs=(VMEM, VMEM),
        compiler_params=SMALL,
        name="repack_p",
    )(got)
    p_mine = to_all(p_send)
    q_send = pl.pallas_call(
        repack_q,
        out_shape=sds(4, 2, 2, TAU, 128),
        in_specs=[SMEM, VMEM],
        out_specs=VMEM,
        compiler_params=SMALL,
        cost_estimate=pl.CostEstimate(flops=0, bytes_accessed=6 * 10**7, transcendentals=0),
        name="repack_q",
    )(me, rest)
    q_mine = [q_send[0]] + [around(q_send[d], d) for d in (1, 2, 3)]
    p_mine, *q_mine = lax.optimization_barrier((p_mine, *q_mine))
    q_all = to_all(copies(jnp.stack(q_mine)))
    p_all = [p_mine] + [around(p_mine, d) for d in (1, 2, 3)]
    p_done = pl.pallas_call(
        p_side,
        out_shape=sds(2, 4, 128, SEQ),
        in_specs=[SMEM] + [VMEM] * 4,
        out_specs=HBM,
        scratch_shapes=[
            pltpu.VMEM((2, SAMPLES, 128), jnp.float32),
            pltpu.VMEM((SAMPLES + 2 * HALF, 256), jnp.bfloat16),
            pltpu.VMEM((2, SEQ, 128), jnp.float32),
            pltpu.VMEM((2, 128, SEQ), jnp.float32),
            pltpu.SemaphoreType.DMA((2,)),
        ],
        compiler_params=pltpu.CompilerParams(vmem_limit_bytes=P_VMEM),
        cost_estimate=pl.CostEstimate(flops=10**9, bytes_accessed=20 * 10**6, transcendentals=0),
        name="p_side",
    )(me, *p_all)
    keep, send = pl.pallas_call(
        correlate,
        out_shape=(sds(4, 8, 2, 16, 128),) * 2,
        in_specs=[SMEM, VMEM, HBM],
        out_specs=(VMEM, VMEM),
        scratch_shapes=[
            pltpu.VMEM((2, SAMPLES, 128), jnp.float32),
            pltpu.VMEM((SAMPLES + 2 * HALF, 256), jnp.bfloat16),
            pltpu.VMEM((2, SEQ, 128), jnp.float32),
            pltpu.VMEM((2, 128, SEQ), jnp.float32),
            pltpu.VMEM((2, 512, K), jnp.bfloat16),
            pltpu.VMEM((2, 512, K), jnp.bfloat16),
            pltpu.VMEM((2, K, 512), jnp.bfloat16),
            pltpu.VMEM((2, K, 512), jnp.bfloat16),
            pltpu.VMEM((512, 512), jnp.float32),
            pltpu.SemaphoreType.DMA((2,)),
        ],
        compiler_params=pltpu.CompilerParams(vmem_limit_bytes=Q_VMEM),
        cost_estimate=pl.CostEstimate(flops=10**10, bytes_accessed=20 * 10**6, transcendentals=0),
        name="correlate",
    )(me, q_all, p_done)
    summed = keep + lax.ppermute(send, "core", [(0, 1), (1, 0)])
    parts = [summed[0]] + [around(summed[d], d) for d in (1, 2, 3)]
    out = pl.pallas_call(
        final_kernel,
        out_shape=sds(LAGS, 16, 128),
        in_specs=[SMEM] + [VMEM] * 4,
        out_specs=VMEM,
        scratch_shapes=[pltpu.VMEM((4, 8, 2, 16, 128), jnp.float32)],
        compiler_params=SMALL,
        name="finish",
    )(me, *parts)
    return jnp.transpose(out, (1, 0, 2))


def solution(mesh):
    grid = Mesh(mesh.devices.reshape(2, 8, 4, 4, 2), ("yh", "z", "x", "yl", "core"))
    in_specs = (P(("yl", "core"), ("yh", "z", "x"), None),)
    out_specs = P(("yh", "z", "x"), None, ("yl", "core"))
    return jax.shard_map(local, mesh=grid, in_specs=in_specs, out_specs=out_specs, check_vma=False)
```

```python
import jax
import jax.numpy as jnp
from jax import lax
from jax.experimental import pallas as pl
from jax.experimental.pallas import tpu as pltpu
from jax.sharding import Mesh, PartitionSpec as P

C = 1024
MAXLAG = 31
HALF = 64
LAGS = 63
SAMPLES = 1536
epsilon = 1e-06

TAU = 24
ROW = SAMPLES + 32
K = 3328
FRONT = 40
QFRONT = FRONT - 24
SEQ = K + 128
CHUNKS = (768, 768, 768, 1024)
ROT = (4, 8, 36, 40)
VMEM = pl.BlockSpec(memory_space=pltpu.VMEM)
HBM = pl.BlockSpec(memory_space=pltpu.HBM)
SMEM = pl.BlockSpec(memory_space=pltpu.SMEM)
P_VMEM = 49 * 1024 * 1024
Q_VMEM = 49 * 1024 * 1024
SMALL = pltpu.CompilerParams(vmem_limit_bytes=8 * 1024 * 1024)


def lanes(shape):
    return lax.broadcasted_iota(jnp.int32, shape, len(shape) - 1)


def prepack(raw, out):
    lane = lanes((TAU, 128))
    for low in range(4):
        a = raw[:, 256 * low : 256 * low + 128]
        b = raw[:, 256 * low + 128 : 256 * low + 256]
        first = jnp.where(
            lane < 32, a, jnp.where(lane < 64, pltpu.roll(b, 32, 1), jnp.where(lane < 96, pltpu.roll(a, 32, 1), pltpu.roll(b, 64, 1)))
        )
        second = jnp.where(
            lane < 32, pltpu.roll(a, 64, 1), jnp.where(lane < 64, pltpu.roll(b, 96, 1), jnp.where(lane < 96, pltpu.roll(a, 96, 1), b))
        )
        for high in range(2):
            out[4 * high + low, :, 512:640] = first
            out[4 * high + low, :, 640:768] = second
            out[4 * high + low, :, 0:512] = raw[:, 512 * high : 512 * high + 512]


def pairs(got, high, pair, at):
    low = lanes((TAU, 128)) < 64
    a = got[4 * high + 2 * pair, :, at : at + 128]
    b = got[4 * high + 2 * pair + 1, :, at : at + 128]
    return jnp.where(low, a, pltpu.roll(b, 64, 1)), jnp.where(low, pltpu.roll(a, 64, 1), b)


def repack(got, p_out, q_out):
    me = lax.axis_index("x")
    for high in range(2):
        for pair in range(2):
            for v in range(4):
                p_out[2 * v, pair, high], p_out[2 * v + 1, pair, high] = pairs(got, high, pair, 128 * v)
            for v in range(2):
                for n, block in enumerate(pairs(got, high, pair, 512 + 128 * v)):
                    q_out[lax.rem(2 * v + n + 4 - me, 4), pair, high] = block


def split(x):
    hi = x.astype(jnp.bfloat16)
    return hi, (x - hi.astype(jnp.float32)).astype(jnp.bfloat16)


def normalize(rec, mag):
    row = lax.broadcasted_iota(jnp.int32, (128, 256), 0)
    col = lanes((128, 256))
    band = jnp.where((col >= row) & (col <= row + 2 * HALF), 1.0, 0.0).astype(jnp.bfloat16)
    zero = jnp.zeros((HALF, 256), jnp.bfloat16)
    mag[0:HALF, :] = zero
    mag[HALF + SAMPLES : 2 * HALF + SAMPLES, :] = zero
    for pair in range(2):
        mean = jnp.sum(rec[pair], axis=0, keepdims=True) * (1.0 / SAMPLES)
        for i in range(12):
            d = rec[pair, 128 * i : 128 * i + 128, :] - mean
            rec[pair, 128 * i : 128 * i + 128, :] = d
            hi, lo = split(jnp.abs(d))
            mag[HALF + 128 * i : HALF + 128 * i + 128, 0:128] = hi
            mag[HALF + 128 * i : HALF + 128 * i + 128, 128:256] = lo
        for i in range(12):
            both = jnp.dot(band, mag[128 * i : 128 * i + 256, :], preferred_element_type=jnp.float32)
            t = lax.broadcasted_iota(jnp.int32, (128, 128), 0) + 128 * i
            count = (jnp.minimum(t, HALF) + jnp.minimum(SAMPLES - 1 - t, HALF) + 1).astype(jnp.float32)
            running = (both[:, 0:128] + both[:, 128:256]) / count
            rec[pair, 128 * i : 128 * i + 128, :] = rec[pair, 128 * i : 128 * i + 128, :] / (running + epsilon)


def place(me, d, high, z):
    return pl.multiple_of(((high * 8 + z) * 4) * TAU + lax.rem(me[0] + 4 - d, 4) * TAU, 8)


def clear(seq):
    seq[0:64, :] = jnp.zeros((64, 128), jnp.float32)
    at = QFRONT + SAMPLES - 16
    seq[at : at + 80, :] = jnp.zeros((80, 128), jnp.float32)
    at = QFRONT + ROW + SAMPLES - 16
    seq[at:SEQ, :] = jnp.zeros((SEQ - at, 128), jnp.float32)


def moves(from_, to, sems, pair, start):
    copy = pltpu.make_async_copy(from_, to, sems.at[pair])
    if start:
        copy.start()
    else:
        copy.wait()


def p_side(me, p0, p1, p2, p3, out, rec, mag, seq, turned, sems):
    for d, ref in enumerate((p0, p1, p2, p3)):
        for high in range(2):
            for z in range(8):
                for pair in range(2):
                    rec[pair, pl.ds(place(me, d, high, z), TAU), :] = ref[z, pair, high]
    normalize(rec, mag)
    for pair in range(2):
        clear(seq.at[pair])
        for i in range(12):
            x = rec[pair, 128 * i : 128 * i + 128, :]
            r = pltpu.roll(x, 64, 1)
            at = FRONT + 128 * i
            seq[pair, at : at + 128, 0:64] = x[:, 0:64]
            seq[pair, at - 16 : at + 112, 64:128] = r[:, 64:128]
            at += ROW
            seq[pair, at : at + 128, 0:64] = r[:, 0:64]
            seq[pair, at - 16 : at + 112, 64:128] = x[:, 64:128]
        for i in range(SEQ // 128):
            turned[pair, :, 128 * i : 128 * i + 128] = seq[pair, 128 * i : 128 * i + 128, :].T
        moves(turned.at[pair], out.at[pair, 0], sems, pair, True)
    for pair in range(2):
        moves(turned.at[pair], out.at[pair, 0], sems, pair, False)


def correlate(me, q_in, p_in, keep, send, rec, mag, seq, turned, lhs_hi, lhs_lo, rhs_hi, rhs_lo, acc, sems):
    for pair in range(2):
        moves(p_in.at[pair, 0], turned.at[pair], sems, pair, True)
    for d in range(4):
        for high in range(2):
            for z in range(8):
                for pair in range(2):
                    rec[pair, pl.ds(place(me, d, high, z), TAU), :] = q_in[z, d, pair, high]
    normalize(rec, mag)
    for pair in range(2):
        clear(seq.at[pair])
        for i in range(12):
            x = rec[pair, 128 * i : 128 * i + 128, :]
            r32, r64, r96 = (pltpu.roll(x, n, 1) for n in (32, 64, 96))
            at = QFRONT + 128 * i
            for e, parts in enumerate(((x, r32, r32, r64), (r64, r96, r96, x))):
                for n, part in enumerate(parts):
                    to = at + e * ROW - 8 * (n % 2)
                    seq[pair, to : to + 128, 32 * n : 32 * n + 32] = part[:, 32 * n : 32 * n + 32]
        moves(p_in.at[pair, 0], turned.at[pair], sems, pair, False)
        start = 0
        for n, width in enumerate(CHUNKS):
            for m in range(8):
                wide = turned[pair, 16 * m : 16 * m + 16, start : start + width + 128]
                for r, rot in enumerate(ROT):
                    hi, lo = split(pltpu.roll(wide, width + 128 - rot, 1)[:, 0:width])
                    lhs_hi[pair, 128 * r + 16 * m : 128 * r + 16 * m + 16, start : start + width] = hi
                    lhs_lo[pair, 128 * r + 16 * m : 128 * r + 16 * m + 16, start : start + width] = lo
            for s in range(4):
                for m in range(width // 128):
                    at = start + 128 * m
                    hi, lo = split(seq[pair, at + s : at + s + 128, :])
                    rhs_hi[pair, at : at + 128, 128 * s : 128 * s + 128] = hi
                    rhs_lo[pair, at : at + 128, 128 * s : 128 * s + 128] = lo
            span = slice(start, start + width)
            part = jnp.dot(lhs_hi[pair, :, span], rhs_hi[pair, span, :], preferred_element_type=jnp.float32)
            part += jnp.dot(lhs_hi[pair, :, span], rhs_lo[pair, span, :], preferred_element_type=jnp.float32)
            part += jnp.dot(lhs_lo[pair, :, span], rhs_hi[pair, span, :], preferred_element_type=jnp.float32)
            if n or pair:
                acc[...] += part
            else:
                acc[...] = part
            start += width
    low = lanes((16, 128)) < 64
    first = me[1] == 0
    for g in range(8):
        for x in range(4):
            at = 64 * g + 16 * x
            for s2 in range(2):
                a = acc[at : at + 16, 256 * s2 : 256 * s2 + 128]
                b = acc[at : at + 16, 256 * s2 + 128 : 256 * s2 + 256]
                one = jnp.where(low, a, pltpu.roll(b, 64, 1))
                two = jnp.where(low, pltpu.roll(a, 64, 1), b)
                keep[x, g, s2] = jnp.where(first, one, two)
                send[x, g, s2] = jnp.where(first, two, one)


def final_kernel(got, out):
    lane = lanes((16, 128))
    for g in range(8):
        r, j = g // 2, g % 2
        r0, r1 = r % 2, r // 2
        for s2 in range(2):
            parts = [got[x, g, s2] for x in range(4)]
            for sb in range(2):
                for i in range(2):
                    mu = 2 * s2 + sb + 4 * (1 - r0) + 8 * i + 16 * (1 - j) + 32 * (1 - r1)
                    if mu == 0:
                        continue
                    n = 2 * sb + i
                    moved = [pltpu.roll(parts[x], (32 * (x - n)) % 128, 1) if x != n else parts[x] for x in range(4)]
                    value = jnp.where(lane < 32, moved[0], jnp.where(lane < 64, moved[1], jnp.where(lane < 96, moved[2], moved[3])))
                    out[mu - 1] = value * (1.0 / SAMPLES)


def sds(*shape, dtype=jnp.float32):
    return jax.ShapeDtypeStruct(shape, dtype)


def around(v, d):
    return lax.ppermute(v, "x", [(i, (i + d) % 4) for i in range(4)])


def copies(v):
    return jnp.broadcast_to(v[None], (8,) + v.shape)


def to_all(v):
    return lax.all_to_all(v, "z", 0, 0, tiled=True)


def local(raw):
    x = lax.axis_index("x")
    me = jnp.stack([x, lax.axis_index("core")]).astype(jnp.int32)
    sent = pl.pallas_call(prepack, out_shape=sds(8, TAU, 768), in_specs=[VMEM], out_specs=VMEM, compiler_params=SMALL, name="prepack")(raw[0])
    got = lax.all_to_all(sent, ("yh", "yl"), 0, 0, tiled=True)
    p_send, q_send = pl.pallas_call(
        repack,
        out_shape=(sds(8, 2, 2, TAU, 128), sds(4, 2, 2, TAU, 128)),
        in_specs=[VMEM],
        out_specs=(VMEM, VMEM),
        compiler_params=SMALL,
        name="repack",
    )(got)
    p_mine = to_all(p_send)
    q_mine = [q_send[0]] + [around(q_send[d], d) for d in (1, 2, 3)]
    p_mine, *q_mine = lax.optimization_barrier((p_mine, *q_mine))
    q_all = to_all(copies(jnp.stack(q_mine)))
    p_all = [p_mine] + [around(p_mine, d) for d in (1, 2, 3)]
    p_done = pl.pallas_call(
        p_side,
        out_shape=sds(2, 4, 128, SEQ),
        in_specs=[SMEM] + [VMEM] * 4,
        out_specs=HBM,
        scratch_shapes=[
            pltpu.VMEM((2, SAMPLES, 128), jnp.float32),
            pltpu.VMEM((SAMPLES + 2 * HALF, 256), jnp.bfloat16),
            pltpu.VMEM((2, SEQ, 128), jnp.float32),
            pltpu.VMEM((2, 128, SEQ), jnp.float32),
            pltpu.SemaphoreType.DMA((2,)),
        ],
        compiler_params=pltpu.CompilerParams(vmem_limit_bytes=P_VMEM),
        cost_estimate=pl.CostEstimate(flops=10**9, bytes_accessed=20 * 10**6, transcendentals=0),
        name="p_side",
    )(me, *p_all)
    keep, send = pl.pallas_call(
        correlate,
        out_shape=(sds(4, 8, 2, 16, 128),) * 2,
        in_specs=[SMEM, VMEM, HBM],
        out_specs=(VMEM, VMEM),
        scratch_shapes=[
            pltpu.VMEM((2, SAMPLES, 128), jnp.float32),
            pltpu.VMEM((SAMPLES + 2 * HALF, 256), jnp.bfloat16),
            pltpu.VMEM((2, SEQ, 128), jnp.float32),
            pltpu.VMEM((2, 128, SEQ), jnp.float32),
            pltpu.VMEM((2, 512, K), jnp.bfloat16),
            pltpu.VMEM((2, 512, K), jnp.bfloat16),
            pltpu.VMEM((2, K, 512), jnp.bfloat16),
            pltpu.VMEM((2, K, 512), jnp.bfloat16),
            pltpu.VMEM((512, 512), jnp.float32),
            pltpu.SemaphoreType.DMA((2,)),
        ],
        compiler_params=pltpu.CompilerParams(vmem_limit_bytes=Q_VMEM),
        cost_estimate=pl.CostEstimate(flops=10**10, bytes_accessed=20 * 10**6, transcendentals=0),
        name="correlate",
    )(me, q_all, p_done)
    summed = keep + lax.ppermute(send, "core", [(0, 1), (1, 0)])
    mine = lax.all_to_all(summed, "x", 0, 0, tiled=True)
    out = pl.pallas_call(final_kernel, out_shape=sds(LAGS, 16, 128), in_specs=[VMEM], out_specs=VMEM, compiler_params=SMALL, name="finish")(mine)
    return jnp.transpose(out, (1, 0, 2))


def solution(mesh):
    grid = Mesh(mesh.devices.reshape(2, 8, 4, 4, 2), ("yh", "z", "x", "yl", "core"))
    in_specs = (P(("yl", "core"), ("yh", "z", "x"), None),)
    out_specs = P(("yh", "z", "x"), None, ("yl", "core"))
    return jax.shard_map(local, mesh=grid, in_specs=in_specs, out_specs=out_specs, check_vma=False)
```
